512 devices in a mesh: gal: 64 (over z, y_lo, core), qry: 8 (over x, y_hi).
Axes of the slice: x: 4, y: 4 (y_hi: 2, y_lo: 2; y = y_hi * 2 + y_lo), z: 16, core: 2. Of those that a mesh axis runs over, the one named last changes fastest.
Arguments:
- gallery: bfloat16 [262144, 768], P('gal'), may hold values from -24 to 24
- bank: bfloat16 [4096, 768], P('qry'), may hold values from -24 to 24
- test: bfloat16 [2048, 768], P('qry'), may hold values from -24 to 24
Outputs:
- normalizers: float32 [262144], P('gal')
- query_lse: float32 [2048], P('qry')
- pooled: float32 [2048, 768], P('qry')
The draws below stay inside these ranges and needn't reach their ends.
All inputs are finite; a program needn't handle non-finite values.
Results may differ from the reference program's by a relative error of at most 0.0003.
Values sent between devices are 32-bit elements; how exact they have to be, the bound alone decides.
A program may use at most 128 MiB of HBM per device.

```python
import math
import jax
import jax.numpy as jnp
from jax import lax

D = 768
GAL_DEV = 4096
GALLERY = 262144
BANK = 4096
TEST = 2048


anchor_count = 8


def anchor_pairs(key):
    shuffled = jax.random.permutation(jax.random.fold_in(key, 12), GALLERY // 2)
    return 2 * shuffled[:2 * anchor_count]


def row_scales(key, count, low_scale, high_scale):
    return jnp.exp(jax.random.uniform(key, (count, 1), jnp.float32, math.log(low_scale), math.log(high_scale)))


def gallery_law(key, low_scale, high_scale):
    base_draw = jnp.clip(jax.random.normal(jax.random.fold_in(key, 11), (GALLERY, D), jnp.float32), -6.0, 6.0)
    shaped = base_draw * row_scales(jax.random.fold_in(key, 15), GALLERY, low_scale, high_scale)
    starts = anchor_pairs(key)
    first_rows = shaped[starts]
    second_rows = shaped[starts + 1]
    return shaped.at[starts].set(first_rows).at[starts + 1].set(second_rows)


def draw_gallery(key, part):
    return gallery_law(key, 1.0, 1.0).astype(jnp.bfloat16)


def draw_bank(key, part):
    key = jax.random.fold_in(key, 2)
    return jnp.clip(jax.random.normal(key, (BANK, D), jnp.float32), -6.0, 6.0).astype(jnp.bfloat16)


def draw_test(key, part):
    key = jax.random.fold_in(key, 3)
    return jnp.clip(jax.random.normal(key, (TEST, D), jnp.float32), -6.0, 6.0).astype(jnp.bfloat16)


def setup_inputs(seed: int = 0) -> dict:
    seeds = jax.random.split(jax.random.key(seed), 4)
    return {
        "gallery": draw_gallery(jax.random.fold_in(seeds[3], 71), 0),
        "bank": draw_bank(jax.random.fold_in(seeds[3], 71), 0),
        "test": draw_test(jax.random.fold_in(seeds[3], 71), 0),
    }


def reference(gallery, bank, test):
    score_scale = 5.0 / math.sqrt(D)
    gallery_blocks = gallery.reshape(GALLERY // GAL_DEV, GAL_DEV, D)

    def bank_block(gallery_rows):
        logits = score_scale * jnp.dot(bank, gallery_rows.T, preferred_element_type=jnp.float32)
        column_peak = lax.optimization_barrier(jnp.max(logits, axis=0))
        return column_peak + jnp.log(lax.optimization_barrier(jnp.sum(jnp.exp(logits - column_peak[None, :]), axis=0)))
    normalizers = lax.map(bank_block, gallery_blocks).reshape(GALLERY)
    norm_blocks = normalizers.reshape(GALLERY // GAL_DEV, GAL_DEV)

    def test_logits(gallery_rows, norm_rows):
        return score_scale * jnp.dot(test, gallery_rows.T, preferred_element_type=jnp.float32) - norm_rows[None, :]

    def block_peak_of(pieces):
        return lax.optimization_barrier(jnp.max(test_logits(pieces[0], pieces[1]), axis=1))
    block_peak = lax.map(block_peak_of, (gallery_blocks, norm_blocks))
    row_max = lax.optimization_barrier(jnp.max(block_peak, axis=0))

    def accumulate(running, pieces):
        peak_now = pieces[2]
        exp_terms = jnp.exp(test_logits(pieces[0], pieces[1]) - peak_now[:, None])
        soft_weights = exp_terms.astype(jnp.bfloat16)
        rescale = jnp.exp(peak_now - row_max)
        block_totals = lax.optimization_barrier(jnp.sum(exp_terms, axis=1))
        block_weighted = jnp.dot(soft_weights, pieces[0], preferred_element_type=jnp.float32)
        totals = running[0] + rescale * block_totals
        weighted = running[1] + rescale[:, None] * block_weighted
        return ((totals, weighted), None)
    start_state = (jnp.zeros((TEST,), jnp.float32), jnp.zeros((TEST, D), jnp.float32))
    (totals, weighted), unused = lax.scan(accumulate, start_state, (gallery_blocks, norm_blocks, block_peak))
    pooled = weighted / totals[:, None]
    query_lse = row_max + jnp.log(totals)
    return (normalizers, query_lse, pooled)
```

```python
import functools
import math

import jax
import jax.numpy as jnp
from jax import lax
from jax.experimental import pallas as pl
from jax.experimental.pallas import tpu as pltpu
from jax.sharding import PartitionSpec as P

MESH = pl.DeviceIdType.MESH
F32 = jnp.float32
BF16 = jnp.bfloat16
LOG2E = math.log2(math.e)
LN2 = math.log(2.0)
NT = (((1,), (1,)), ((), ()))
CLIPS, BANKQ, TESTQ, D = 4096, 512, 256, 768
PARTS = 4
PC = CLIPS // PARTS
PR = PC // 128
FAR = (4, 3, 5, 2, 6, 1, 7)


def kernel(
    gallery, bank, test, norm_out, lse_out, pooled_out,
    gal, bnk, tst, raw, wts, nloc, nrecv, n2, work, crecv, csum, s1recv, s1sum, s2recv, final,
    sc0, sc0r, sc1, sc1r, sc2, sc2r, lsef, e0, e1, e2,
    lsem, osem, nsem, rsem, nsend, ssem,
):
    me, q = lax.axis_index("gal"), lax.axis_index("qry")
    z, y, c = me // 4, (me // 2) % 2, me % 2
    zp, h = z % 2, z // 2
    g = y * 2 + zp

    def at(z_, y_, c_):
        return {"gal": z_ * 4 + y_ * 2 + c_}

    sib = at(z, y, 1 - c)
    zf, yf = z + 1 - 2 * zp, 1 - y
    quad = {
        1: (at(zf, y, c), y * 2 + 1 - zp),
        2: (at(z, yf, c), yf * 2 + zp),
        3: (at(zf, yf, c), yf * 2 + 1 - zp),
    }
    ring = {d: (at(((h + d) % 8) * 2 + zp, y, c), (h + d) % 8) for d in range(1, 8)}
    panel = {d: {"qry": (q + d) % 8} for d in range(1, 8)}

    loads = [pltpu.make_async_copy(bank, bnk, lsem.at[PARTS])]
    for j in range(PARTS):
        rows = pl.ds(j * PC, PC)
        loads.append(pltpu.make_async_copy(gallery.at[rows], gal.at[rows], lsem.at[j]))
    loads.append(pltpu.make_async_copy(test, tst, lsem.at[PARTS + 1]))
    for load in loads:
        load.start()

    barrier = pltpu.get_barrier_semaphore()
    peers = [sib] + [p for p, _ in quad.values()] + [p for p, _ in ring.values()] + list(panel.values())
    for p in peers:
        pl.semaphore_signal(barrier, inc=1, device_id=p, device_id_type=MESH)

    def send(src, dst, stage, k, device):
        pltpu.make_async_remote_copy(
            src_ref=src, dst_ref=dst, send_sem=ssem.at[stage, k], recv_sem=rsem.at[stage, k],
            device_id=device, device_id_type=MESH,
        ).start()

    def arrived(ref, stage, k):
        pltpu.make_async_copy(ref, ref, rsem.at[stage, k]).wait()

    c2 = 5.0 / math.sqrt(D) * LOG2E
    loads[0].wait()

    def bank_part(j, carry):
        rows = pl.ds(pl.multiple_of(j * PC, PC), PC)
        pltpu.make_async_copy(gallery.at[rows], gal.at[rows], lsem.at[j]).wait()
        r = lax.dot_general(bnk[...], gal[rows, :], NT, preferred_element_type=F32)
        m = jnp.max(r, axis=0, keepdims=True)
        s = jnp.sum(jnp.exp2((r - m) * c2), axis=0, keepdims=True)
        l2 = m * c2 + jnp.log(s) * LOG2E
        for i in range(PR):
            nloc[pl.ds(j * PR + i, 1), :] = l2[:, i * 128 : (i + 1) * 128]

        @pl.when(j == 0)
        def _():
            pl.semaphore_wait(barrier, len(peers))

        block = pl.ds(pl.multiple_of(j * PR, PR), PR)
        for d in FAR:
            pltpu.make_async_remote_copy(
                src_ref=nloc.at[block], dst_ref=nrecv.at[d - 1, block],
                send_sem=nsend.at[j], recv_sem=nsem.at[j],
                device_id=panel[d], device_id_type=MESH,
            ).start()
        return carry

    lax.fori_loop(0, PARTS, bank_part, 0)

    loads[-1].wait()

    def test_part(j, carry):
        rows = pl.ds(pl.multiple_of(j * 1024, 1024), 1024)
        raw[:, rows] = lax.dot_general(tst[...], gal[rows, :], NT, preferred_element_type=F32)
        return carry

    lax.fori_loop(0, CLIPS // 1024, test_part, 0)

    def norm_part(j, peak):
        block = pl.ds(pl.multiple_of(j * PR, PR), PR)
        part = nrecv.at[:, block]
        pltpu.make_async_copy(part, part, nsem.at[j]).wait()
        own = nloc[block, :]
        m = own
        for d in range(7):
            m = jnp.maximum(m, nrecv[d, block, :])
        s = jnp.exp2(own - m)
        for d in range(7):
            s = s + jnp.exp2(nrecv[d, block, :] - m)
        n2[block, :] = m + jnp.log(s) * LOG2E

        def shift(i, peak):
            lanes = pl.ds(pl.multiple_of((j * PR + i) * 128, 128), 128)
            x = raw[:, lanes] * c2 - n2[pl.ds(j * PR + i, 1), :]
            raw[:, lanes] = x
            return jnp.maximum(peak, x)

        return lax.fori_loop(0, PR, shift, peak, unroll=2)

    peak = lax.fori_loop(0, PARTS, norm_part, jnp.full((TESTQ, 128), -jnp.inf, F32))
    peak = jnp.max(peak, axis=1, keepdims=True)
    norm_out[...] = n2[...] * LN2

    def weigh(i, total):
        lanes = pl.ds(pl.multiple_of(i * 128, 128), 128)
        e = jnp.exp2(raw[:, lanes] - peak)
        wts[:, lanes] = e.astype(BF16)
        return total + e

    total = lax.fori_loop(0, CLIPS // 128, weigh, jnp.zeros((TESTQ, 128), F32), unroll=2)
    total = jnp.sum(total, axis=1, keepdims=True)

    def packed(m, t):
        lane = lax.broadcasted_iota(jnp.int32, m.shape, 1)
        return jnp.where(lane < 64, m, t)

    def spread(a, lane):
        return jnp.broadcast_to(a[:, lane : lane + 1], a.shape)

    def merged(tiles, scales):
        ms, ts = [spread(a, 0) for a in tiles], [spread(a, 64) for a in tiles]
        m = functools.reduce(jnp.maximum, ms)
        t = None
        for i, (mi, ti) in enumerate(zip(ms, ts)):
            e = jnp.exp2(mi - m)
            scales[i] = e
            t = e * ti if t is None else t + e * ti
        return m, t

    sc0[...] = packed(jnp.broadcast_to(peak, (TESTQ, 128)), jnp.broadcast_to(total, (TESTQ, 128)))
    send(sc0, sc0r, 0, 3, sib)

    def pool(tile):
        lanes = pl.ds(pl.multiple_of(tile * 256, 256), 256)
        out = jnp.dot(wts[...], gal[:, lanes], preferred_element_type=F32)
        work[2 * tile] = out[:, :128]
        work[2 * tile + 1] = out[:, 128:]

    pool(2 * (1 - c))
    send(work.at[pl.ds(4 * (1 - c), 2)], crecv.at[pl.ds(1, 2)], 0, 1, sib)
    arrived(sc0r, 0, 3)
    m, t = merged([sc0[...], sc0r[...]], e0)
    sc1[...] = packed(m, t)
    for r in (3, 1, 2):
        device, gp = quad[r]
        send(sc1.at[pl.ds(gp * 64, 64)], sc1r.at[r - 1], 1, 3, device)
    pool(1)
    send(work.at[3 - c], crecv.at[0], 0, 0, sib)
    pool(2 * c)

    own = (2 + c, 4 * c, 4 * c + 1)
    for k in range(3):
        if k == 0:
            arrived(crecv.at[0], 0, 0)
        if k == 1:
            arrived(crecv.at[pl.ds(1, 2)], 0, 1)
        csum[k] = e0[0] * work[own[k]] + e0[1] * crecv[k]
        for r in (3, 1, 2):
            device, gp = quad[r]
            send(csum.at[k, pl.ds(gp * 64, 64)], s1recv.at[r - 1, k], 1, k, device)

    rows64 = pl.ds(pl.multiple_of(g * 64, 64), 64)
    rows8 = pl.ds(pl.multiple_of(h * 8, 8), 8)
    rows = pl.ds(pl.multiple_of(g * 64 + h * 8, 8), 8)
    arrived(sc1r, 1, 3)
    m, t = merged([sc1[rows64, :]] + [sc1r[i] for i in range(3)], e1)
    sc2[...] = packed(m, t)
    for d in FAR:
        device, hp = ring[d]
        send(sc2.at[pl.ds(hp * 8, 8)], sc2r.at[d - 1], 2, 3, device)

    for k in range(3):
        arrived(s1recv.at[:, k], 1, k)
        acc = e1[0] * csum[k, rows64, :]
        for i in range(3):
            acc = acc + e1[i + 1] * s1recv[i, k]
        s1sum[k] = acc
        for d in FAR:
            device, hp = ring[d]
            send(s1sum.at[k, pl.ds(hp * 8, 8)], s2recv.at[d - 1, k], 2, k, device)

    arrived(sc2r, 2, 3)
    m, t = merged([sc2[rows8, :]] + [sc2r[i] for i in range(7)], e2)
    lsef[rows, :] = m * LN2 + jnp.log(t)
    for d in FAR:
        send(lsef.at[rows], lsef.at[rows], 3, 3, ring[d][0])
    inv = 1.0 / t
    for k in range(3):
        arrived(s2recv.at[:, k], 2, k)
        acc = e2[0] * s1sum[k, rows8, :]
        for i in range(7):
            acc = acc + e2[i + 1] * s2recv[i, k]
        final[own[k], rows, :] = acc * inv
        for d in FAR:
            send(final.at[own[k], rows], final.at[own[k], rows], 3, k, ring[d][0])

    arrived(sc2r, 3, 3)
    for r in (3, 1, 2):
        send(lsef.at[rows64], lsef.at[rows64], 4, 3, quad[r][0])
    for k in range(3):
        arrived(s2recv.at[:, k], 3, k)
        for r in (3, 1, 2):
            send(final.at[own[k], rows64], final.at[own[k], rows64], 4, k, quad[r][0])

    arrived(sc1r, 4, 3)
    sub = lax.broadcasted_iota(jnp.int32, (128, 128), 0)
    lane = lax.broadcasted_iota(jnp.int32, (128, 128), 1)
    for i in range(2):
        tile = lsef[i * 128 : (i + 1) * 128, :]
        lse_out[i : i + 1, :] = jnp.sum(jnp.where(sub == lane, tile, 0.0), axis=0, keepdims=True)

    def store(b, k):
        return pltpu.make_async_copy(
            final.at[b], pooled_out.at[:, pl.ds(pl.multiple_of(b * 128, 128), 128)], osem.at[k]
        )

    for k in range(3):
        arrived(s1recv.at[:, k], 4, k)
        send(final.at[own[k]], final.at[own[k]], 5, k, sib)
        store(own[k], k).start()
    other = (3 - c, 4 * (1 - c), 4 * (1 - c) + 1)
    for k in range(3):
        arrived(crecv.at[k], 5, k)
        store(other[k], 3 + k).start()
    for k in range(3):
        store(own[k], k).wait()
        store(other[k], 3 + k).wait()

    def sent(ref, stage, k):
        pltpu.make_async_copy(ref, ref, ssem.at[stage, k]).wait()

    for j in range(PARTS):
        part = nrecv.at[:, j * PR : (j + 1) * PR]
        pltpu.make_async_copy(part, part, nsend.at[j]).wait()
    sent(sc0r, 0, 3)
    sent(crecv.at[pl.ds(1, 2)], 0, 1)
    sent(crecv.at[0], 0, 0)
    sent(sc1r, 1, 3)
    sent(sc2r, 2, 3)
    sent(sc2r, 3, 3)
    sent(sc1r, 4, 3)
    for k in range(3):
        sent(s1recv.at[:, k], 1, k)
        sent(s2recv.at[:, k], 2, k)
        sent(s2recv.at[:, k], 3, k)
        sent(s1recv.at[:, k], 4, k)
        sent(crecv.at[k], 5, k)


def body(gallery, bank, test):
    vm = pltpu.VMEM
    dma = pltpu.SemaphoreType.DMA
    norm, lse, pooled = pl.pallas_call(
        kernel,
        out_shape=(
            jax.ShapeDtypeStruct((CLIPS // 128, 128), F32),
            jax.ShapeDtypeStruct((TESTQ // 128, 128), F32),
            jax.ShapeDtypeStruct((TESTQ, D), F32),
        ),
        in_specs=[pl.BlockSpec(memory_space=pl.ANY)] * 3,
        out_specs=(
            pl.BlockSpec(memory_space=pltpu.VMEM),
            pl.BlockSpec(memory_space=pltpu.VMEM),
            pl.BlockSpec(memory_space=pl.ANY),
        ),
        scratch_shapes=[
            vm((CLIPS, D), BF16),
            vm((BANKQ, D), BF16),
            vm((TESTQ, D), BF16),
            vm((TESTQ, CLIPS), F32),
            vm((TESTQ, CLIPS), BF16),
            vm((CLIPS // 128, 128), F32),
            vm((7, CLIPS // 128, 128), F32),
            vm((CLIPS // 128, 128), F32),
            vm((6, TESTQ, 128), F32),
            vm((3, TESTQ, 128), F32),
            vm((3, TESTQ, 128), F32),
            vm((3, 3, 64, 128), F32),
            vm((3, 64, 128), F32),
            vm((7, 3, 8, 128), F32),
            vm((6, TESTQ, 128), F32),
            vm((TESTQ, 128), F32),
            vm((TESTQ, 128), F32),
            vm((TESTQ, 128), F32),
            vm((3, 64, 128), F32),
            vm((64, 128), F32),
            vm((7, 8, 128), F32),
            vm((TESTQ, 128), F32),
            vm((2, TESTQ, 128), F32),
            vm((4, 64, 128), F32),
            vm((8, 8, 128), F32),
            dma((PARTS + 2,)),
            dma((6,)),
            dma((PARTS,)),
            dma((6, 4)),
            dma((PARTS,)),
            dma((6, 4)),
        ],
        compiler_params=pltpu.CompilerParams(
            collective_id=0, has_side_effects=True, vmem_limit_bytes=48 * 2**20
        ),
    )(gallery, bank, test)
    return norm.reshape(CLIPS), lse.reshape(TESTQ), pooled


def solution(mesh):
    placed = (P("gal", None), P("qry", None), P("qry", None))
    return jax.shard_map(
        body,
        mesh=mesh,
        in_specs=placed,
        out_specs=(P("gal"), P("qry"), P("qry", None)),
        check_vma=False,
    )
```

```python
import functools
import math

import jax
import jax.numpy as jnp
from jax import lax
from jax.experimental import pallas as pl
from jax.experimental.pallas import tpu as pltpu
from jax.sharding import PartitionSpec as P

MESH = pl.DeviceIdType.MESH
F32 = jnp.float32
BF16 = jnp.bfloat16
LOG2E = math.log2(math.e)
LN2 = math.log(2.0)
NT = (((1,), (1,)), ((), ()))
CLIPS, BANKQ, TESTQ, D = 4096, 512, 256, 768
PARTS = 4
PC = CLIPS // PARTS
PR = PC // 128
SPAN = (pl.ds(0, CLIPS // 128 - PR), pl.ds(CLIPS // 128 - PR, PR))
FAR = (4, 3, 5, 2, 6, 1, 7)
NEAR = (0, 1, 7, 2, 6, 3, 5, 4)
QUAD_IN, RING_OUT, QUAD_OUT = 9, 17, 25


def kernel(
    gallery, bank, test, norm_out, lse_out, pooled_out,
    gal, bnk, tst, raw, wts, nloc, nrecv, n2, work, crecv, csum, s1recv, s1sum, s2recv, final,
    sc0, sc0r, sc1, sc1r, sc2, sc2r, lsef, e0, e1, e2,
    lsem, osem, nsem, rsem, nsend, ssem,
):
    me, q = lax.axis_index("gal"), lax.axis_index("qry")
    z, y, c = me // 4, (me // 2) % 2, me % 2
    zp, h = z % 2, z // 2
    g = y * 2 + zp

    def at(z_, y_, c_):
        return {"gal": z_ * 4 + y_ * 2 + c_}

    sib = at(z, y, 1 - c)
    zf, yf = z + 1 - 2 * zp, 1 - y
    quad = {
        1: (at(zf, y, c), y * 2 + 1 - zp),
        2: (at(z, yf, c), yf * 2 + zp),
        3: (at(zf, yf, c), yf * 2 + 1 - zp),
    }
    ring = {d: (at(((h + d) % 8) * 2 + zp, y, c), (h + d) % 8) for d in range(1, 8)}
    panel = {d: {"qry": (q + d) % 8} for d in range(1, 8)}

    loads = [pltpu.make_async_copy(bank, bnk, lsem.at[PARTS])]
    for j in range(PARTS):
        rows = pl.ds(j * PC, PC)
        loads.append(pltpu.make_async_copy(gallery.at[rows], gal.at[rows], lsem.at[j]))
    loads.append(pltpu.make_async_copy(test, tst, lsem.at[PARTS + 1]))
    for load in loads:
        load.start()

    barrier = pltpu.get_barrier_semaphore()
    peers = [sib] + [p for p, _ in quad.values()] + [p for p, _ in ring.values()] + list(panel.values())
    for p in peers:
        pl.semaphore_signal(barrier, inc=1, device_id=p, device_id_type=MESH)

    def send(src, dst, stage, slot, device):
        pltpu.make_async_remote_copy(
            src_ref=src, dst_ref=dst, send_sem=ssem.at[stage], recv_sem=rsem.at[slot],
            device_id=device, device_id_type=MESH,
        ).start()

    def arrived(ref, slot):
        pltpu.make_async_copy(ref, ref, rsem.at[slot]).wait()

    c2 = 5.0 / math.sqrt(D) * LOG2E
    loads[0].wait()

    def bank_part(j, carry):
        rows = pl.ds(pl.multiple_of(j * PC, PC), PC)
        pltpu.make_async_copy(gallery.at[rows], gal.at[rows], lsem.at[j]).wait()
        r = lax.dot_general(bnk[...], gal[rows, :], NT, preferred_element_type=F32)
        m = jnp.max(r, axis=0, keepdims=True)
        s = jnp.sum(jnp.exp2((r - m) * c2), axis=0, keepdims=True)
        l2 = m * c2 + jnp.log(s) * LOG2E
        for i in range(PR):
            nloc[pl.ds(j * PR + i, 1), :] = l2[:, i * 128 : (i + 1) * 128]
        return carry

    def send_part(i):
        for d in FAR:
            pltpu.make_async_remote_copy(
                src_ref=nloc.at[SPAN[i]], dst_ref=nrecv.at[d - 1, SPAN[i]],
                send_sem=nsend.at[i], recv_sem=nsem.at[i],
                device_id=panel[d], device_id_type=MESH,
            ).start()

    lax.fori_loop(0, PARTS - 1, bank_part, 0)
    pl.semaphore_wait(barrier, len(peers))
    send_part(0)
    bank_part(PARTS - 1, 0)
    send_part(1)

    loads[-1].wait()

    def test_part(j, carry):
        rows = pl.ds(pl.multiple_of(j * 1024, 1024), 1024)
        raw[:, rows] = lax.dot_general(tst[...], gal[rows, :], NT, preferred_element_type=F32)
        return carry

    lax.fori_loop(0, CLIPS // 1024, test_part, 0)

    peak = jnp.full((TESTQ, 128), -jnp.inf, F32)
    for i, block in enumerate(SPAN):
        part = nrecv.at[:, block]
        pltpu.make_async_copy(part, part, nsem.at[i]).wait()
        own = nloc[block, :]
        m = own
        for d in range(7):
            m = jnp.maximum(m, nrecv[d, block, :])
        s = jnp.exp2(own - m)
        for d in range(7):
            s = s + jnp.exp2(nrecv[d, block, :] - m)
        n2[block, :] = m + jnp.log(s) * LOG2E

        def shift(i, peak):
            lanes = pl.ds(pl.multiple_of(i * 128, 128), 128)
            x = raw[:, lanes] * c2 - n2[pl.ds(i, 1), :]
            raw[:, lanes] = x
            return jnp.maximum(peak, x)

        peak = lax.fori_loop(block.start, block.start + block.size, shift, peak, unroll=2)
    peak = jnp.max(peak, axis=1, keepdims=True)
    norm_out[...] = n2[...] * LN2

    def weigh(i, total):
        lanes = pl.ds(pl.multiple_of(i * 128, 128), 128)
        e = jnp.exp2(raw[:, lanes] - peak)
        wts[:, lanes] = e.astype(BF16)
        return total + e

    total = lax.fori_loop(0, CLIPS // 128, weigh, jnp.zeros((TESTQ, 128), F32), unroll=2)
    total = jnp.sum(total, axis=1, keepdims=True)

    def packed(m, t):
        lane = lax.broadcasted_iota(jnp.int32, m.shape, 1)
        return jnp.where(lane < 64, m, t)

    def spread(a, lane):
        return jnp.broadcast_to(a[:, lane : lane + 1], a.shape)

    def merged(tiles, scales):
        ms, ts = [spread(a, 0) for a in tiles], [spread(a, 64) for a in tiles]
        m = functools.reduce(jnp.maximum, ms)
        t = None
        for i, (mi, ti) in enumerate(zip(ms, ts)):
            e = jnp.exp2(mi - m)
            scales[i] = e
            t = e * ti if t is None else t + e * ti
        return m, t

    sc0[...] = packed(jnp.broadcast_to(peak, (TESTQ, 128)), jnp.broadcast_to(total, (TESTQ, 128)))
    send(sc0, sc0r, 0, 0, sib)

    def pool(tile):
        lanes = pl.ds(pl.multiple_of(tile * 256, 256), 256)
        out = jnp.dot(wts[...], gal[:, lanes], preferred_element_type=F32)
        work[2 * tile] = out[:, :128]
        work[2 * tile + 1] = out[:, 128:]

    mid, outer = 2 - 2 * c, c
    pool(2 * (1 - c))
    send(work.at[pl.ds(4 * (1 - c), 2)], crecv.at[pl.ds(1 - c, 2)], 1, 1, sib)
    arrived(sc0r, 0)
    m, t = merged([sc0[...], sc0r[...]], e0)
    sc1[...] = packed(m, t)
    for r in (3, 1, 2):
        device, gp = quad[r]
        send(sc1.at[pl.ds(gp * 64, 64)], sc1r.at[r - 1], 2, 3, device)
    pool(1)
    send(work.at[3 - c], crecv.at[2 * c], 1, 2, sib)
    pool(2 * c)

    def core_sum(k, b):
        both = e0[0] * work[b] + e0[1] * crecv[k]
        csum[k] = both.reshape(4, 8, 8, 128)

    arrived(crecv.at[pl.ds(outer, 2)], 1)
    for i in range(2):
        core_sum(outer + i, 4 * c + i)
    arrived(crecv.at[mid], 2)
    core_sum(mid, 2 + c)

    for d in FAR + (0,):
        for r in (3, 1, 2):
            device, gp = quad[r]
            send(csum.at[:, gp, (h + d) % 8], s1recv.at[r - 1, d], 3, QUAD_IN + d, device)

    arrived(sc1r, 3)
    m, t = merged([sc1[pl.ds(pl.multiple_of(g * 64, 64), 64), :]] + [sc1r[i] for i in range(3)], e1)
    sc2[...] = packed(m, t)
    for d in FAR:
        device, hp = ring[d]
        send(sc2.at[pl.ds(hp * 8, 8)], sc2r.at[d - 1], 4, 4, device)

    for d in FAR + (0,):
        hp = (h + d) % 8
        rows = pl.ds(pl.multiple_of(hp * 8, 8), 8)
        arrived(s1recv.at[:, d], QUAD_IN + d)
        acc = e1[0, rows, :] * csum[:, g, hp]
        for i in range(3):
            acc = acc + e1[i + 1, rows, :] * s1recv[i, d]
        s1sum[d] = acc
        if d:
            send(s1sum.at[d], s2recv.at[d - 1], 5, 5, ring[d][0])

    arrived(sc2r, 4)
    rows8 = pl.ds(pl.multiple_of(h * 8, 8), 8)
    m, t = merged([sc2[rows8, :]] + [sc2r[i] for i in range(7)], e2)
    lsef[g, h] = m * LN2 + jnp.log(t)
    for d in FAR:
        send(lsef.at[g, h], lsef.at[g, h], 6, 6, ring[d][0])
    inv = 1.0 / t
    mine = pl.ds(3 * c, 3)
    arrived(s2recv, 5)
    acc = e2[0] * s1sum[0]
    for i in range(7):
        acc = acc + e2[i + 1] * s2recv[i]
    final[mine, g, h] = acc * inv
    for d in FAR:
        send(final.at[mine, g, h], final.at[mine, g, h], 7, RING_OUT + d, ring[d][0])

    for d in NEAR:
        hp = (h - d + 8) % 8
        if d:
            arrived(s2recv.at[0], RING_OUT + d)
        piece = final.at[mine, g, hp]
        for r in (3, 1, 2):
            send(piece, piece, 8, QUAD_OUT + d, quad[r][0])
        if d == 6:
            arrived(sc2r, 6)
            for r in (3, 1, 2):
                send(lsef.at[g], lsef.at[g], 9, 7, quad[r][0])

    for d in NEAR:
        hp = (h - d + 8) % 8
        arrived(s1recv.at[:, 0], QUAD_OUT + d)
        send(final.at[mine, :, hp], final.at[mine, :, hp], 10, 8, sib)

    def store(b, k):
        lanes = pl.ds(pl.multiple_of(b * 128, 128), 128)
        return pltpu.make_async_copy(final.at[b], pooled_out.at[:, :, :, lanes], osem.at[k])

    for k in range(3):
        store(3 * c + k, k).start()
    arrived(sc1r, 7)
    sub = lax.broadcasted_iota(jnp.int32, (128, 128), 0)
    lane = lax.broadcasted_iota(jnp.int32, (128, 128), 1)
    for i in range(2):
        tile = lsef[2 * i : 2 * i + 2].reshape(128, 128)
        lse_out[i : i + 1, :] = jnp.sum(jnp.where(sub == lane, tile, 0.0), axis=0, keepdims=True)
    arrived(crecv, 8)
    for k in range(3):
        store(3 - 3 * c + k, 3 + k).start()
    for k in range(3):
        store(3 * c + k, k).wait()
        store(3 - 3 * c + k, 3 + k).wait()

    for i, block in enumerate(SPAN):
        part = nrecv.at[:, block]
        pltpu.make_async_copy(part, part, nsend.at[i]).wait()
    for stage, ref in enumerate((sc0r, crecv, sc1r, s1recv, sc2r, s2recv, sc2r, s2recv, s1recv, sc1r, crecv)):
        pltpu.make_async_copy(ref, ref, ssem.at[stage]).wait()


def write(norm, lse, pooled, norm_out, lse_out, pooled_out):
    norm_out[...] = norm[...]
    lse_out[...] = lse[...]
    pooled_out[...] = pooled[...]


def body(gallery, bank, test):
    vm = pltpu.VMEM
    dma = pltpu.SemaphoreType.DMA
    norm, lse, pooled = pl.pallas_call(
        kernel,
        out_shape=(
            jax.ShapeDtypeStruct((CLIPS // 128, 128), F32),
            jax.ShapeDtypeStruct((TESTQ // 128, 128), F32),
            jax.ShapeDtypeStruct((4, 8, 8, D), F32),
        ),
        in_specs=[pl.BlockSpec(memory_space=pl.ANY)] * 3,
        out_specs=(
            pl.BlockSpec(memory_space=pltpu.VMEM),
            pl.BlockSpec(memory_space=pltpu.VMEM),
            pl.BlockSpec(memory_space=pl.ANY),
        ),
        scratch_shapes=[
            vm((CLIPS, D), BF16),
            vm((BANKQ, D), BF16),
            vm((TESTQ, D), BF16),
            vm((TESTQ, CLIPS), F32),
            vm((TESTQ, CLIPS), BF16),
            vm((CLIPS // 128, 128), F32),
            vm((7, CLIPS // 128, 128), F32),
            vm((CLIPS // 128, 128), F32),
            vm((6, TESTQ, 128), F32),
            vm((3, TESTQ, 128), F32),
            vm((3, 4, 8, 8, 128), F32),
            vm((3, 8, 3, 8, 128), F32),
            vm((8, 3, 8, 128), F32),
            vm((7, 3, 8, 128), F32),
            vm((6, 4, 8, 8, 128), F32),
            vm((TESTQ, 128), F32),
            vm((TESTQ, 128), F32),
            vm((TESTQ, 128), F32),
            vm((3, 64, 128), F32),
            vm((64, 128), F32),
            vm((7, 8, 128), F32),
            vm((4, 8, 8, 128), F32),
            vm((2, TESTQ, 128), F32),
            vm((4, 64, 128), F32),
            vm((8, 8, 128), F32),
            dma((PARTS + 2,)),
            dma((6,)),
            dma((2,)),
            dma((33,)),
            dma((2,)),
            dma((11,)),
        ],
        compiler_params=pltpu.CompilerParams(
            collective_id=0, has_side_effects=True, vmem_limit_bytes=62 * 2**20
        ),
    )(gallery, bank, test)
    norm, lse, pooled = pl.pallas_call(
        write,
        out_shape=tuple(jax.ShapeDtypeStruct(a.shape, F32) for a in (norm, lse, pooled)),
        in_specs=[pl.BlockSpec(memory_space=pltpu.VMEM)] * 3,
        out_specs=(pl.BlockSpec(memory_space=pltpu.VMEM),) * 3,
    )(norm, lse, pooled)
    return norm.reshape(CLIPS), lse.reshape(TESTQ), pooled.reshape(TESTQ, D)


def solution(mesh):
    placed = (P("gal", None), P("qry", None), P("qry", None))
    return jax.shard_map(
        body,
        mesh=mesh,
        in_specs=placed,
        out_specs=(P("gal"), P("qry"), P("qry", None)),
        check_vma=False,
    )
```

```python
import functools
import math

import jax
import jax.numpy as jnp
from jax import lax
from jax.experimental import pallas as pl
from jax.experimental.pallas import tpu as pltpu
from jax.sharding import PartitionSpec as P

MESH = pl.DeviceIdType.MESH
F32 = jnp.float32
BF16 = jnp.bfloat16
LOG2E = math.log2(math.e)
LN2 = math.log(2.0)
NT = (((1,), (1,)), ((), ()))
CLIPS, BANKQ, TESTQ, D = 4096, 512, 256, 768
PARTS = 4
PC = CLIPS // PARTS
PR = PC // 128
SPAN = (pl.ds(0, CLIPS // 128 - PR), pl.ds(CLIPS // 128 - PR, PR))
QUAD_IN, RING_OUT, QUAD_OUT = 9, 17, 25


def kernel(
    gallery, bank, test, norm_out, lse_out, final,
    gal, bnk, tst, raw, wts, nloc, nrecv, n2, work, crecv, csum, s1recv, s1sum, s2recv,
    sc0, sc0r, sc1, sc1r, sc2, sc2r, lsef, e0, e1, e2,
    lsem, nsem, rsem, nsend, ssem,
):
    me, q = lax.axis_index("gal"), lax.axis_index("qry")
    z, y, c = me // 4, (me // 2) % 2, me % 2
    zp, h = z % 2, z // 2
    g = y * 2 + zp

    def at(z_, y_, c_):
        return {"gal": z_ * 4 + y_ * 2 + c_}

    sib = at(z, y, 1 - c)
    zf, yf = z + 1 - 2 * zp, 1 - y
    quad = {
        1: (at(zf, y, c), y * 2 + 1 - zp),
        2: (at(z, yf, c), yf * 2 + zp),
        3: (at(zf, yf, c), yf * 2 + 1 - zp),
    }

    def ring(d):
        return at(((h + d) % 8) * 2 + zp, y, c)

    def panel(d):
        return {"qry": (q + d) % 8}

    def distance(i):
        return 4 + (i + 1) // 2 * (1 - 2 * (i % 2))

    def each(n, step):
        def run(i, carry):
            step(i)
            return carry

        lax.fori_loop(0, n, run, 0)

    loads = [pltpu.make_async_copy(bank, bnk, lsem.at[PARTS])]
    for j in range(PARTS):
        rows = pl.ds(j * PC, PC)
        loads.append(pltpu.make_async_copy(gallery.at[rows], gal.at[rows], lsem.at[j]))
    loads.append(pltpu.make_async_copy(test, tst, lsem.at[PARTS + 1]))
    for load in loads:
        load.start()

    barrier = pltpu.get_barrier_semaphore()

    def greet(device):
        pl.semaphore_signal(barrier, inc=1, device_id=device, device_id_type=MESH)

    def greet_far(i):
        greet(ring(distance(i)))
        greet(panel(distance(i)))

    each(7, greet_far)
    for device in [sib] + [p for p, _ in quad.values()]:
        greet(device)

    def send(src, dst, stage, slot, device):
        pltpu.make_async_remote_copy(
            src_ref=src, dst_ref=dst, send_sem=ssem.at[stage], recv_sem=rsem.at[slot],
            device_id=device, device_id_type=MESH,
        ).start()

    def arrived(ref, slot):
        pltpu.make_async_copy(ref, ref, rsem.at[slot]).wait()

    c2 = 5.0 / math.sqrt(D) * LOG2E
    loads[0].wait()

    def send_part(i):
        def step(k):
            d = distance(k)
            pltpu.make_async_remote_copy(
                src_ref=nloc.at[SPAN[i]], dst_ref=nrecv.at[d - 1, SPAN[i]],
                send_sem=nsend.at[i], recv_sem=nsem.at[i],
                device_id=panel(d), device_id_type=MESH,
            ).start()

        each(7, step)

    def bank_part(j, carry):
        rows = pl.ds(pl.multiple_of(j * PC, PC), PC)
        pltpu.make_async_copy(gallery.at[rows], gal.at[rows], lsem.at[j]).wait()
        r = lax.dot_general(bnk[...], gal[rows, :], NT, preferred_element_type=F32)
        m = jnp.max(r, axis=0, keepdims=True)
        s = jnp.sum(jnp.exp2((r - m) * c2), axis=0, keepdims=True)
        l2 = m * c2 + jnp.log(s) * LOG2E
        for i in range(PR):
            nloc[pl.ds(j * PR + i, 1), :] = l2[:, i * 128 : (i + 1) * 128]

        @pl.when(j == PARTS - 2)
        def _():
            pl.semaphore_wait(barrier, 18)
            send_part(0)

        return carry

    lax.fori_loop(0, PARTS, bank_part, 0)
    send_part(1)

    loads[-1].wait()

    def test_part(j, carry):
        rows = pl.ds(pl.multiple_of(j * 1024, 1024), 1024)
        raw[:, rows] = lax.dot_general(tst[...], gal[rows, :], NT, preferred_element_type=F32)
        return carry

    lax.fori_loop(0, CLIPS // 1024, test_part, 0)

    peak = jnp.full((TESTQ, 128), -jnp.inf, F32)
    for i, block in enumerate(SPAN):
        part = nrecv.at[:, block]
        pltpu.make_async_copy(part, part, nsem.at[i]).wait()
        own = nloc[block, :]
        m = own
        for d in range(7):
            m = jnp.maximum(m, nrecv[d, block, :])
        s = jnp.exp2(own - m)
        for d in range(7):
            s = s + jnp.exp2(nrecv[d, block, :] - m)
        n2[block, :] = m + jnp.log(s) * LOG2E

        def shift(i, peak):
            lanes = pl.ds(pl.multiple_of(i * 128, 128), 128)
            x = raw[:, lanes] * c2 - n2[pl.ds(i, 1), :]
            raw[:, lanes] = x
            return jnp.maximum(peak, x)

        peak = lax.fori_loop(block.start, block.start + block.size, shift, peak, unroll=2)
    peak = jnp.max(peak, axis=1, keepdims=True)
    norm_out[...] = n2[...] * LN2

    def weigh(i, total):
        lanes = pl.ds(pl.multiple_of(i * 128, 128), 128)
        e = jnp.exp2(raw[:, lanes] - peak)
        wts[:, lanes] = e.astype(BF16)
        return total + e

    total = lax.fori_loop(0, CLIPS // 128, weigh, jnp.zeros((TESTQ, 128), F32), unroll=2)
    total = jnp.sum(total, axis=1, keepdims=True)

    def packed(m, t):
        lane = lax.broadcasted_iota(jnp.int32, m.shape, 1)
        return jnp.where(lane < 64, m, t)

    def spread(a, lane):
        return jnp.broadcast_to(a[:, lane : lane + 1], a.shape)

    def merged(tiles, scales):
        ms, ts = [spread(a, 0) for a in tiles], [spread(a, 64) for a in tiles]
        m = functools.reduce(jnp.maximum, ms)
        t = None
        for i, (mi, ti) in enumerate(zip(ms, ts)):
            e = jnp.exp2(mi - m)
            scales[i] = e
            t = e * ti if t is None else t + e * ti
        return m, t

    sc0[...] = packed(jnp.broadcast_to(peak, (TESTQ, 128)), jnp.broadcast_to(total, (TESTQ, 128)))
    send(sc0, sc0r, 0, 0, sib)

    mid, outer = 2 - 2 * c, c

    def pool(i, carry):
        tile = 2 - 2 * c + i * (2 * c - 1)
        lanes = pl.ds(pl.multiple_of(tile * 256, 256), 256)
        out = jnp.dot(wts[...], gal[:, lanes], preferred_element_type=F32)
        work[2 * tile] = out[:, :128]
        work[2 * tile + 1] = out[:, 128:]

        @pl.when(i == 0)
        def _():
            send(work.at[pl.ds(4 * (1 - c), 2)], crecv.at[pl.ds(1 - c, 2)], 1, 1, sib)

        @pl.when(i == 1)
        def _():
            send(work.at[3 - c], crecv.at[2 * c], 1, 2, sib)
            arrived(sc0r, 0)
            m, t = merged([sc0[...], sc0r[...]], e0)
            sc1[...] = packed(m, t)
            for r in (3, 1, 2):
                device, gp = quad[r]
                send(sc1.at[pl.ds(gp * 64, 64)], sc1r.at[r - 1], 2, 3, device)

        return carry

    lax.fori_loop(0, 3, pool, 0)

    def core_sum(k, b):
        both = e0[0] * work[b] + e0[1] * crecv[k]
        csum[k] = both.reshape(4, 8, 8, 128)

    arrived(crecv.at[pl.ds(outer, 2)], 1)
    for i in range(2):
        core_sum(outer + i, 4 * c + i)
    arrived(crecv.at[mid], 2)
    core_sum(mid, 2 + c)

    def quad_in(i):
        d = distance(i)
        for r in (3, 1, 2):
            device, gp = quad[r]
            send(csum.at[:, gp, (h + d) % 8], s1recv.at[r - 1, d], 3, QUAD_IN + d, device)

    each(8, quad_in)
    arrived(sc1r, 3)
    m, t = merged([sc1[pl.ds(pl.multiple_of(g * 64, 64), 64), :]] + [sc1r[i] for i in range(3)], e1)
    sc2[...] = packed(m, t)

    def scalars_in(i):
        d = distance(i)
        rows = pl.ds(pl.multiple_of((h + d) % 8 * 8, 8), 8)
        send(sc2.at[rows], sc2r.at[d - 1], 4, 4, ring(d))

    each(7, scalars_in)

    def quad_sum(d):
        hp = (h + d) % 8
        rows = pl.ds(pl.multiple_of(hp * 8, 8), 8)
        arrived(s1recv.at[:, d], QUAD_IN + d)
        acc = e1[0, rows, :] * csum[:, g, hp]
        for i in range(3):
            acc = acc + e1[i + 1, rows, :] * s1recv[i, d]
        s1sum[d] = acc

    def ring_in(i):
        d = distance(i)
        quad_sum(d)
        send(s1sum.at[d], s2recv.at[d - 1], 5, 5, ring(d))

    each(7, ring_in)
    quad_sum(0)

    arrived(sc2r, 4)
    rows8 = pl.ds(pl.multiple_of(h * 8, 8), 8)
    m, t = merged([sc2[rows8, :]] + [sc2r[i] for i in range(7)], e2)
    lsef[g, h] = m * LN2 + jnp.log(t)
    each(7, lambda i: send(lsef.at[g, h], lsef.at[g, h], 6, 6, ring(distance(i))))
    inv = 1.0 / t
    mine = pl.ds(3 * c, 3)
    arrived(s2recv, 5)
    acc = e2[0] * s1sum[0]
    for i in range(7):
        acc = acc + e2[i + 1] * s2recv[i]
    final[mine, g, h] = acc * inv
    piece = final.at[mine, g, h]
    each(7, lambda i: send(piece, piece, 7, RING_OUT + distance(i), ring(distance(i))))

    def quad_out(d):
        piece = final.at[mine, g, (h - d + 8) % 8]
        for r in (3, 1, 2):
            send(piece, piece, 8, QUAD_OUT + d, quad[r][0])

    def ring_out(i):
        d = distance(6 - i)
        arrived(s2recv.at[0], RING_OUT + d)
        quad_out(d)

    quad_out(0)
    each(7, ring_out)
    arrived(sc2r, 6)
    for r in (3, 1, 2):
        send(lsef.at[g], lsef.at[g], 9, 7, quad[r][0])

    def sibling_out(i):
        d = distance(7 - i)
        arrived(s1recv.at[:, 0], QUAD_OUT + d)
        piece = final.at[mine, :, (h - d + 8) % 8]
        send(piece, piece, 10, 8, sib)

    each(8, sibling_out)

    arrived(sc1r, 7)
    sub = lax.broadcasted_iota(jnp.int32, (128, 128), 0)
    lane = lax.broadcasted_iota(jnp.int32, (128, 128), 1)
    for i in range(2):
        tile = lsef[2 * i : 2 * i + 2].reshape(128, 128)
        lse_out[i : i + 1, :] = jnp.sum(jnp.where(sub == lane, tile, 0.0), axis=0, keepdims=True)
    arrived(crecv, 8)

    for i, block in enumerate(SPAN):
        part = nrecv.at[:, block]
        pltpu.make_async_copy(part, part, nsend.at[i]).wait()
    for stage, ref in enumerate((sc0r, crecv, sc1r, s1recv, sc2r, s2recv, sc2r, s2recv, s1recv, sc1r, crecv)):
        pltpu.make_async_copy(ref, ref, ssem.at[stage]).wait()


def write(norm, lse, parts, norm_out, lse_out, pooled_out, sem):
    copies = [
        pltpu.make_async_copy(parts.at[b], pooled_out.at[:, :, :, pl.ds(b * 128, 128)], sem.at[b])
        for b in range(6)
    ]
    copies.append(pltpu.make_async_copy(norm, norm_out, sem.at[6]))
    copies.append(pltpu.make_async_copy(lse, lse_out, sem.at[7]))
    for copy in copies:
        copy.start()
    for copy in copies:
        copy.wait()


def body(gallery, bank, test):
    vm = pltpu.VMEM
    dma = pltpu.SemaphoreType.DMA
    norm, lse, parts = pl.pallas_call(
        kernel,
        out_shape=(
            vm((CLIPS // 128, 128), F32),
            vm((TESTQ // 128, 128), F32),
            vm((6, 4, 8, 8, 128), F32),
        ),
        in_specs=[pl.BlockSpec(memory_space=pl.ANY)] * 3,
        out_specs=(pl.BlockSpec(memory_space=pltpu.VMEM),) * 3,
        scratch_shapes=[
            vm((CLIPS, D), BF16),
            vm((BANKQ, D), BF16),
            vm((TESTQ, D), BF16),
            vm((TESTQ, CLIPS), F32),
            vm((TESTQ, CLIPS), BF16),
            vm((CLIPS // 128, 128), F32),
            vm((7, CLIPS // 128, 128), F32),
            vm((CLIPS // 128, 128), F32),
            vm((6, TESTQ, 128), F32),
            vm((3, TESTQ, 128), F32),
            vm((3, 4, 8, 8, 128), F32),
            vm((3, 8, 3, 8, 128), F32),
            vm((8, 3, 8, 128), F32),
            vm((7, 3, 8, 128), F32),
            vm((TESTQ, 128), F32),
            vm((TESTQ, 128), F32),
            vm((TESTQ, 128), F32),
            vm((3, 64, 128), F32),
            vm((64, 128), F32),
            vm((7, 8, 128), F32),
            vm((4, 8, 8, 128), F32),
            vm((2, TESTQ, 128), F32),
            vm((4, 64, 128), F32),
            vm((8, 8, 128), F32),
            dma((PARTS + 2,)),
            dma((2,)),
            dma((33,)),
            dma((2,)),
            dma((11,)),
        ],
        compiler_params=pltpu.CompilerParams(
            collective_id=0, has_side_effects=True, vmem_limit_bytes=52 * 2**20
        ),
    )(*(pltpu.with_memory_space_constraint(a, pltpu.HBM) for a in (gallery, bank, test)))
    norm, lse, pooled = pl.pallas_call(
        write,
        out_shape=tuple(jax.ShapeDtypeStruct(s, F32) for s in (norm.shape, lse.shape, (4, 8, 8, D))),
        in_specs=[pl.BlockSpec(memory_space=pltpu.VMEM)] * 3,
        out_specs=(pl.BlockSpec(memory_space=pl.ANY),) * 3,
        scratch_shapes=[dma((8,))],
        compiler_params=pltpu.CompilerParams(vmem_limit_bytes=8 * 2**20),
    )(*(pltpu.with_memory_space_constraint(a, pltpu.VMEM) for a in (norm, lse, parts)))
    return norm.reshape(CLIPS), lse.reshape(TESTQ), pooled.reshape(TESTQ, D)


def solution(mesh):
    placed = (P("gal", None), P("qry", None), P("qry", None))
    return jax.shard_map(
        body,
        mesh=mesh,
        in_specs=placed,
        out_specs=(P("gal"), P("qry"), P("qry", None)),
        check_vma=False,
    )
```

```python
import functools
import math

import jax
import jax.numpy as jnp
from jax import lax
from jax.experimental import pallas as pl
from jax.experimental.pallas import tpu as pltpu
from jax.sharding import PartitionSpec as P

MESH = pl.DeviceIdType.MESH
F32 = jnp.float32
BF16 = jnp.bfloat16
LOG2E = math.log2(math.e)
LN2 = math.log(2.0)
NT = (((1,), (1,)), ((), ()))
CLIPS, BANKQ, TESTQ, D = 4096, 512, 256, 768
PARTS = 4
PC = CLIPS // PARTS
PR = PC // 128
SPAN = (pl.ds(0, CLIPS // 128 - PR), pl.ds(CLIPS // 128 - PR, PR))
QUAD_IN, RING_OUT, QUAD_OUT = 9, 17, 25


def kernel(
    gallery, bank, test, norm_out, lse_out, final,
    gal, bnk, tst, raw, wts, nloc, nrecv, n2, work, crecv, csum, s1recv, s1sum, s2recv,
    sc0, sc0r, sc1, sc1n, sc1r, sc2, sc2r, lsef, lsen, e0, e1, e2,
    lsem, nsem, rsem, nsend, ssem,
):
    me, q = lax.axis_index("gal"), lax.axis_index("qry")
    z, y, c = me // 4, (me // 2) % 2, me % 2
    zp, h = z % 2, z // 2
    g = y * 2 + zp

    def at(z_, y_, c_):
        return {"gal": z_ * 4 + y_ * 2 + c_}

    sib = at(z, y, 1 - c)
    zf, yf = z + 1 - 2 * zp, 1 - y
    quad = {
        1: (at(zf, y, c), y * 2 + 1 - zp),
        2: (at(z, yf, c), yf * 2 + zp),
        3: (at(zf, yf, c), yf * 2 + 1 - zp),
    }

    def ring(d):
        return at(((h + d) % 8) * 2 + zp, y, c)

    def panel(d):
        return {"qry": (q + d) % 8}

    def distance(i):
        return 4 + (i + 1) // 2 * (1 - 2 * (i % 2))

    def each(n, step):
        def run(i, carry):
            step(i)
            return carry

        lax.fori_loop(0, n, run, 0)

    loads = [pltpu.make_async_copy(bank, bnk, lsem.at[PARTS])]
    for j in range(PARTS):
        rows = pl.ds(j * PC, PC)
        loads.append(pltpu.make_async_copy(gallery.at[rows], gal.at[rows], lsem.at[j]))
    loads.append(pltpu.make_async_copy(test, tst, lsem.at[PARTS + 1]))
    for load in loads:
        load.start()

    barrier = pltpu.get_barrier_semaphore()

    def greet(device):
        pl.semaphore_signal(barrier, inc=1, device_id=device, device_id_type=MESH)

    def greet_far(i):
        greet(ring(distance(i)))
        greet(panel(distance(i)))

    each(7, greet_far)
    for device in [sib] + [p for p, _ in quad.values()]:
        greet(device)

    def send(src, dst, stage, slot, device):
        pltpu.make_async_remote_copy(
            src_ref=src, dst_ref=dst, send_sem=ssem.at[stage], recv_sem=rsem.at[slot],
            device_id=device, device_id_type=MESH,
        ).start()

    def arrived(ref, slot):
        pltpu.make_async_copy(ref, ref, rsem.at[slot]).wait()

    c2 = 5.0 / math.sqrt(D) * LOG2E
    loads[0].wait()

    def send_part(i):
        def step(k):
            d = distance(k)
            pltpu.make_async_remote_copy(
                src_ref=nloc.at[SPAN[i]], dst_ref=nrecv.at[d - 1, SPAN[i]],
                send_sem=nsend.at[i], recv_sem=nsem.at[i],
                device_id=panel(d), device_id_type=MESH,
            ).start()

        each(7, step)

    def bank_part(j, carry):
        rows = pl.ds(pl.multiple_of(j * PC, PC), PC)
        pltpu.make_async_copy(gallery.at[rows], gal.at[rows], lsem.at[j]).wait()
        r = lax.dot_general(bnk[...], gal[rows, :], NT, preferred_element_type=F32)
        m = jnp.max(r, axis=0, keepdims=True)
        s = jnp.sum(jnp.exp2((r - m) * c2), axis=0, keepdims=True)
        l2 = m * c2 + jnp.log(s) * LOG2E
        for i in range(PR):
            nloc[pl.ds(j * PR + i, 1), :] = l2[:, i * 128 : (i + 1) * 128]

        @pl.when(j == PARTS - 2)
        def _():
            pl.semaphore_wait(barrier, 18)
            send_part(0)

        return carry

    lax.fori_loop(0, PARTS, bank_part, 0)
    send_part(1)

    loads[-1].wait()

    def test_part(j, carry):
        rows = pl.ds(pl.multiple_of(j * 2048, 2048), 2048)
        raw[:, rows] = lax.dot_general(tst[...], gal[rows, :], NT, preferred_element_type=F32)
        return carry

    lax.fori_loop(0, CLIPS // 2048, test_part, 0)

    peak = jnp.full((TESTQ, 128), -jnp.inf, F32)
    for i, block in enumerate(SPAN):
        part = nrecv.at[:, block]
        pltpu.make_async_copy(part, part, nsem.at[i]).wait()
        own = nloc[block, :]
        m = own
        for d in range(7):
            m = jnp.maximum(m, nrecv[d, block, :])
        s = jnp.exp2(own - m)
        for d in range(7):
            s = s + jnp.exp2(nrecv[d, block, :] - m)
        n2[block, :] = m + jnp.log(s) * LOG2E

        def shift(i, peak):
            lanes = pl.ds(pl.multiple_of(i * 128, 128), 128)
            x = raw[:, lanes] * c2 - n2[pl.ds(i, 1), :]
            raw[:, lanes] = x
            return jnp.maximum(peak, x)

        peak = lax.fori_loop(block.start, block.start + block.size, shift, peak, unroll=2)
    peak = jnp.max(peak, axis=1, keepdims=True)
    norm_out[...] = n2[...] * LN2

    def weigh(i, total):
        lanes = pl.ds(pl.multiple_of(i * 128, 128), 128)
        e = jnp.exp2(raw[:, lanes] - peak)
        wts[:, lanes] = e.astype(BF16)
        return total + e

    total = lax.fori_loop(0, CLIPS // 128, weigh, jnp.zeros((TESTQ, 128), F32), unroll=2)
    total = jnp.sum(total, axis=1, keepdims=True)

    def packed(m, t):
        lane = lax.broadcasted_iota(jnp.int32, m.shape, 1)
        return jnp.where(lane < 64, m, t)

    def spread(a, lane):
        return jnp.broadcast_to(a[:, lane : lane + 1], a.shape)

    def merged(pairs, scales):
        m = functools.reduce(jnp.maximum, [mi for mi, _ in pairs])
        t = None
        for i, (mi, ti) in enumerate(pairs):
            e = jnp.exp2(mi - m)
            scales[i] = e
            t = e * ti if t is None else t + e * ti
        return m, t

    def pair(tile):
        return spread(tile, 0), spread(tile, 64)

    sub = lax.broadcasted_iota(jnp.int32, (64, 128), 0)
    lane = lax.broadcasted_iota(jnp.int32, (64, 128), 1)

    def narrow(tile):
        hit = (lane == sub) | (lane == sub + 64)
        return jnp.broadcast_to(jnp.sum(jnp.where(hit, tile, 0.0), axis=0, keepdims=True), (8, 128))

    def wide(row):
        def column(shift):
            x = jnp.where(lane == sub + shift, jnp.broadcast_to(row, (64, 128)), 0.0)
            return jnp.broadcast_to(jnp.sum(x, axis=1, keepdims=True), (64, 128))

        return column(0), column(64)

    sc0[...] = packed(jnp.broadcast_to(peak, (TESTQ, 128)), jnp.broadcast_to(total, (TESTQ, 128)))
    send(sc0, sc0r, 0, 0, sib)

    mid, outer = 2 - 2 * c, c

    def pool(i, carry):
        tile = 2 - 2 * c + i * (2 * c - 1)
        lanes = pl.ds(pl.multiple_of(tile * 256, 256), 256)
        out = jnp.dot(wts[...], gal[:, lanes], preferred_element_type=F32)
        work[2 * tile] = out[:, :128]
        work[2 * tile + 1] = out[:, 128:]

        @pl.when(i == 0)
        def _():
            send(work.at[pl.ds(4 * (1 - c), 2)], crecv.at[pl.ds(1 - c, 2)], 1, 1, sib)

        @pl.when(i == 1)
        def _():
            send(work.at[3 - c], crecv.at[2 * c], 1, 2, sib)
            arrived(sc0r, 0)
            m, t = merged([pair(sc0[...]), pair(sc0r[...])], e0)
            sc1[...] = packed(m, t)
            for k in range(4):
                sc1n[k] = narrow(sc1[k * 64 : (k + 1) * 64, :])
            for r in (3, 1, 2):
                device, gp = quad[r]
                send(sc1n.at[gp], sc1r.at[r - 1], 2, 3, device)

        return carry

    lax.fori_loop(0, 3, pool, 0)

    def core_sum(k, b):
        both = e0[0] * work[b] + e0[1] * crecv[k]
        csum[k] = both.reshape(4, 8, 8, 128)

    arrived(crecv.at[pl.ds(outer, 2)], 1)
    for i in range(2):
        core_sum(outer + i, 4 * c + i)
    arrived(crecv.at[mid], 2)
    core_sum(mid, 2 + c)

    def quad_in(i):
        d = distance(i)
        for r in (3, 1, 2):
            device, gp = quad[r]
            send(csum.at[:, gp, (h + d) % 8], s1recv.at[r - 1, d], 3, QUAD_IN + d, device)

    each(8, quad_in)
    arrived(sc1r, 3)
    m, t = merged([pair(sc1[pl.ds(pl.multiple_of(g * 64, 64), 64), :])] + [wide(sc1r[i, :1, :]) for i in range(3)], e1)
    sc2[...] = packed(m, t)

    def scalars_in(i):
        d = distance(i)
        rows = pl.ds(pl.multiple_of((h + d) % 8 * 8, 8), 8)
        send(sc2.at[rows], sc2r.at[d - 1], 4, 4, ring(d))

    each(7, scalars_in)

    def quad_sum(d):
        hp = (h + d) % 8
        rows = pl.ds(pl.multiple_of(hp * 8, 8), 8)
        arrived(s1recv.at[:, d], QUAD_IN + d)
        acc = e1[0, rows, :] * csum[:, g, hp]
        for i in range(3):
            acc = acc + e1[i + 1, rows, :] * s1recv[i, d]
        s1sum[d] = acc

    def ring_in(i):
        d = distance(i)
        quad_sum(d)
        send(s1sum.at[d], s2recv.at[d - 1], 5, 5, ring(d))

    each(7, ring_in)
    quad_sum(0)

    arrived(sc2r, 4)
    rows8 = pl.ds(pl.multiple_of(h * 8, 8), 8)
    m, t = merged([pair(sc2[rows8, :])] + [pair(sc2r[i]) for i in range(7)], e2)
    lsef[g, h] = m * LN2 + jnp.log(t)
    each(7, lambda i: send(lsef.at[g, h], lsef.at[g, h], 6, 6, ring(distance(i))))
    inv = 1.0 / t
    mine = pl.ds(3 * c, 3)
    arrived(s2recv, 5)
    acc = e2[0] * s1sum[0]
    for i in range(7):
        acc = acc + e2[i + 1] * s2recv[i]
    final[mine, g, h] = acc * inv
    piece = final.at[mine, g, h]
    each(7, lambda i: send(piece, piece, 7, RING_OUT + distance(i), ring(distance(i))))

    def quad_out(d):
        piece = final.at[mine, g, (h - d + 8) % 8]
        for r in (3, 1, 2):
            send(piece, piece, 8, QUAD_OUT + d, quad[r][0])

    def ring_out(i):
        d = distance(6 - i)
        arrived(s2recv.at[0], RING_OUT + d)
        quad_out(d)

    quad_out(0)
    each(7, ring_out)
    arrived(sc2r, 6)
    lsen[g] = narrow(lsef[g].reshape(64, 128))
    for r in (3, 1, 2):
        send(lsen.at[g], lsen.at[g], 9, 7, quad[r][0])

    def sibling_out(i):
        d = distance(7 - i)
        arrived(s1recv.at[:, 0], QUAD_OUT + d)
        piece = final.at[mine, :, (h - d + 8) % 8]
        send(piece, piece, 10, 8, sib)

    each(8, sibling_out)

    arrived(sc1r, 7)
    for i in range(2):
        low = lane[:1] < 64
        lse_out[i : i + 1, :] = jnp.where(low, lsen[2 * i, :1, :], lsen[2 * i + 1, :1, :])
    arrived(crecv, 8)

    for i, block in enumerate(SPAN):
        part = nrecv.at[:, block]
        pltpu.make_async_copy(part, part, nsend.at[i]).wait()
    for stage, ref in enumerate((sc0r, crecv, sc1r, s1recv, sc2r, s2recv, sc2r, s2recv, s1recv, sc1r, crecv)):
        pltpu.make_async_copy(ref, ref, ssem.at[stage]).wait()


def write(norm, lse, parts, norm_out, lse_out, pooled_out, sem):
    copies = [
        pltpu.make_async_copy(parts.at[b], pooled_out.at[:, :, :, pl.ds(b * 128, 128)], sem.at[b])
        for b in range(6)
    ]
    copies.append(pltpu.make_async_copy(norm, norm_out, sem.at[6]))
    copies.append(pltpu.make_async_copy(lse, lse_out, sem.at[7]))
    for copy in copies:
        copy.start()
    for copy in copies:
        copy.wait()


def body(gallery, bank, test):
    vm = pltpu.VMEM
    dma = pltpu.SemaphoreType.DMA
    norm, lse, parts = pl.pallas_call(
        kernel,
        out_shape=(
            vm((CLIPS // 128, 128), F32),
            vm((TESTQ // 128, 128), F32),
            vm((6, 4, 8, 8, 128), F32),
        ),
        in_specs=[pl.BlockSpec(memory_space=pl.ANY)] * 3,
        out_specs=(pl.BlockSpec(memory_space=pltpu.VMEM),) * 3,
        scratch_shapes=[
            vm((CLIPS, D), BF16),
            vm((BANKQ, D), BF16),
            vm((TESTQ, D), BF16),
            vm((TESTQ, CLIPS), F32),
            vm((TESTQ, CLIPS), BF16),
            vm((CLIPS // 128, 128), F32),
            vm((7, CLIPS // 128, 128), F32),
            vm((CLIPS // 128, 128), F32),
            vm((6, TESTQ, 128), F32),
            vm((3, TESTQ, 128), F32),
            vm((3, 4, 8, 8, 128), F32),
            vm((3, 8, 3, 8, 128), F32),
            vm((8, 3, 8, 128), F32),
            vm((7, 3, 8, 128), F32),
            vm((TESTQ, 128), F32),
            vm((TESTQ, 128), F32),
            vm((TESTQ, 128), F32),
            vm((4, 8, 128), F32),
            vm((3, 8, 128), F32),
            vm((64, 128), F32),
            vm((7, 8, 128), F32),
            vm((4, 8, 8, 128), F32),
            vm((4, 8, 128), F32),
            vm((2, TESTQ, 128), F32),
            vm((4, 64, 128), F32),
            vm((8, 8, 128), F32),
            dma((PARTS + 2,)),
            dma((2,)),
            dma((33,)),
            dma((2,)),
            dma((11,)),
        ],
        compiler_params=pltpu.CompilerParams(
            collective_id=0, has_side_effects=True, vmem_limit_bytes=52 * 2**20
        ),
    )(*(pltpu.with_memory_space_constraint(a, pltpu.HBM) for a in (gallery, bank, test)))
    norm, lse, pooled = pl.pallas_call(
        write,
        out_shape=tuple(jax.ShapeDtypeStruct(s, F32) for s in (norm.shape, lse.shape, (4, 8, 8, D))),
        in_specs=[pl.BlockSpec(memory_space=pltpu.VMEM)] * 3,
        out_specs=(pl.BlockSpec(memory_space=pl.ANY),) * 3,
        scratch_shapes=[dma((8,))],
        compiler_params=pltpu.CompilerParams(vmem_limit_bytes=8 * 2**20),
    )(*(pltpu.with_memory_space_constraint(a, pltpu.VMEM) for a in (norm, lse, parts)))
    return norm.reshape(CLIPS), lse.reshape(TESTQ), pooled.reshape(TESTQ, D)


def solution(mesh):
    placed = (P("gal", None), P("qry", None), P("qry", None))
    return jax.shard_map(
        body,
        mesh=mesh,
        in_specs=placed,
        out_specs=(P("gal"), P("qry"), P("qry", None)),
        check_vma=False,
    )
```

```python
import functools
import math

import jax
import jax.numpy as jnp
from jax import lax
from jax.experimental import pallas as pl
from jax.experimental.pallas import tpu as pltpu
from jax.sharding import PartitionSpec as P

MESH = pl.DeviceIdType.MESH
F32 = jnp.float32
BF16 = jnp.bfloat16
LOG2E = math.log2(math.e)
LN2 = math.log(2.0)
NT = (((1,), (1,)), ((), ()))
CLIPS, BANKQ, TESTQ, D = 4096, 512, 256, 768
PARTS = 4
PC = CLIPS // PARTS
PR = PC // 128
SPAN = (pl.ds(0, CLIPS // 128 - PR), pl.ds(CLIPS // 128 - PR, PR))
QUAD_IN, RING_OUT, QUAD_OUT = 9, 17, 25


def kernel(
    gallery, bank, test, norm_out, lse_out, final,
    gal, bnk, tst, raw, wts, nloc, nrecv, n2, work, crecv, csum, s1recv, s1sum, s2recv,
    sc0, sc0r, sc1, sc1n, sc1r, sc2, sc2r, lse_own, lser, lsen, e0, e1, e2,
    lsem, nsem, rsem, nsend, ssem,
):
    me, q = lax.axis_index("gal"), lax.axis_index("qry")
    z, y, c = me // 4, (me // 2) % 2, me % 2
    zp, h = z % 2, z // 2
    g = y * 2 + zp

    def at(z_, y_, c_):
        return {"gal": z_ * 4 + y_ * 2 + c_}

    sib = at(z, y, 1 - c)
    zf, yf = z + 1 - 2 * zp, 1 - y
    quad = {
        1: (at(zf, y, c), y * 2 + 1 - zp),
        2: (at(z, yf, c), yf * 2 + zp),
        3: (at(zf, yf, c), yf * 2 + 1 - zp),
    }

    def ring(d):
        return at(((h + d) % 8) * 2 + zp, y, c)

    def panel(d):
        return {"qry": (q + d) % 8}

    def distance(i):
        return 4 + (i + 1) // 2 * (1 - 2 * (i % 2))

    def each(n, step):
        def run(i, carry):
            step(i)
            return carry

        lax.fori_loop(0, n, run, 0)

    loads = [pltpu.make_async_copy(bank, bnk, lsem.at[PARTS])]
    for j in range(PARTS):
        rows = pl.ds(j * PC, PC)
        loads.append(pltpu.make_async_copy(gallery.at[rows], gal.at[rows], lsem.at[j]))
    loads.append(pltpu.make_async_copy(test, tst, lsem.at[PARTS + 1]))
    for load in loads:
        load.start()

    barrier = pltpu.get_barrier_semaphore()

    def greet(device):
        pl.semaphore_signal(barrier, inc=1, device_id=device, device_id_type=MESH)

    def greet_far(i):
        greet(ring(distance(i)))
        greet(panel(distance(i)))

    each(7, greet_far)
    for device in [sib] + [p for p, _ in quad.values()]:
        greet(device)

    def send(src, dst, stage, slot, device):
        pltpu.make_async_remote_copy(
            src_ref=src, dst_ref=dst, send_sem=ssem.at[stage], recv_sem=rsem.at[slot],
            device_id=device, device_id_type=MESH,
        ).start()

    def arrived(ref, slot):
        pltpu.make_async_copy(ref, ref, rsem.at[slot]).wait()

    c2 = 5.0 / math.sqrt(D) * LOG2E
    loads[0].wait()

    def send_part(i):
        def step(k):
            d = distance(k)
            pltpu.make_async_remote_copy(
                src_ref=nloc.at[SPAN[i]], dst_ref=nrecv.at[d - 1, SPAN[i]],
                send_sem=nsend.at[i], recv_sem=nsem.at[i],
                device_id=panel(d), device_id_type=MESH,
            ).start()

        each(7, step)

    def bank_part(j, carry):
        rows = pl.ds(pl.multiple_of(j * PC, PC), PC)
        pltpu.make_async_copy(gallery.at[rows], gal.at[rows], lsem.at[j]).wait()
        r = lax.dot_general(bnk[...], gal[rows, :], NT, preferred_element_type=F32)
        m = jnp.max(r, axis=0, keepdims=True)
        s = jnp.sum(jnp.exp2((r - m) * c2), axis=0, keepdims=True)
        l2 = m * c2 + jnp.log(s) * LOG2E
        for i in range(PR):
            nloc[pl.ds(j * PR + i, 1), :] = l2[:, i * 128 : (i + 1) * 128]

        @pl.when(j == PARTS - 2)
        def _():
            pl.semaphore_wait(barrier, 18)
            send_part(0)

        return carry

    lax.fori_loop(0, PARTS, bank_part, 0)
    send_part(1)

    loads[-1].wait()

    def test_part(j, carry):
        rows = pl.ds(pl.multiple_of(j * 2048, 2048), 2048)
        raw[:, rows] = lax.dot_general(tst[...], gal[rows, :], NT, preferred_element_type=F32)
        return carry

    lax.fori_loop(0, CLIPS // 2048, test_part, 0)

    peak = jnp.full((TESTQ, 128), -jnp.inf, F32)
    for i, block in enumerate(SPAN):
        part = nrecv.at[:, block]
        pltpu.make_async_copy(part, part, nsem.at[i]).wait()
        own = nloc[block, :]
        m = own
        for d in range(7):
            m = jnp.maximum(m, nrecv[d, block, :])
        s = jnp.exp2(own - m)
        for d in range(7):
            s = s + jnp.exp2(nrecv[d, block, :] - m)
        n2[block, :] = m + jnp.log(s) * LOG2E

        def shift(i, peak):
            lanes = pl.ds(pl.multiple_of(i * 128, 128), 128)
            x = raw[:, lanes] * c2 - n2[pl.ds(i, 1), :]
            raw[:, lanes] = x
            return jnp.maximum(peak, x)

        peak = lax.fori_loop(block.start, block.start + block.size, shift, peak, unroll=2)
    peak = jnp.max(peak, axis=1, keepdims=True)
    norm_out[...] = n2[...] * LN2

    def weigh(i, total):
        lanes = pl.ds(pl.multiple_of(i * 128, 128), 128)
        e = jnp.exp2(raw[:, lanes] - peak)
        wts[:, lanes] = e.astype(BF16)
        return total + e

    total = lax.fori_loop(0, CLIPS // 128, weigh, jnp.zeros((TESTQ, 128), F32), unroll=2)
    total = jnp.sum(total, axis=1, keepdims=True)

    def packed(m, t):
        lane = lax.broadcasted_iota(jnp.int32, m.shape, 1)
        return jnp.where(lane < 64, m, t)

    def spread(a, lane):
        return jnp.broadcast_to(a[:, lane : lane + 1], a.shape)

    def merged(pairs, scales):
        m = functools.reduce(jnp.maximum, [mi for mi, _ in pairs])
        t = None
        for i, (mi, ti) in enumerate(pairs):
            e = jnp.exp2(mi - m)
            scales[i] = e
            t = e * ti if t is None else t + e * ti
        return m, t

    def pair(tile):
        return spread(tile, 0), spread(tile, 64)

    sub = lax.broadcasted_iota(jnp.int32, (64, 128), 0)
    lane = lax.broadcasted_iota(jnp.int32, (64, 128), 1)

    def narrow(tile):
        hit = (lane == sub) | (lane == sub + 64)
        return jnp.sum(jnp.where(hit, tile, 0.0), axis=0, keepdims=True)

    def wide(row, first, count):
        spot = first + lax.broadcasted_iota(jnp.int32, (count, 128), 0)

        def column(shift):
            x = jnp.where(lane[:count] == spot + shift, jnp.broadcast_to(row, (count, 128)), 0.0)
            return jnp.broadcast_to(jnp.sum(x, axis=1, keepdims=True), (count, 128))

        return column(0), column(64)

    sc0[...] = packed(jnp.broadcast_to(peak, (TESTQ, 128)), jnp.broadcast_to(total, (TESTQ, 128)))
    send(sc0, sc0r, 0, 0, sib)

    mid, outer = 2 - 2 * c, c

    def pool(i, carry):
        tile = 2 - 2 * c + i * (2 * c - 1)
        lanes = pl.ds(pl.multiple_of(tile * 256, 256), 256)
        out = jnp.dot(wts[...], gal[:, lanes], preferred_element_type=F32)
        work[2 * tile] = out[:, :128]
        work[2 * tile + 1] = out[:, 128:]

        @pl.when(i == 0)
        def _():
            send(work.at[pl.ds(4 * (1 - c), 2)], crecv.at[pl.ds(1 - c, 2)], 1, 1, sib)

        @pl.when(i == 1)
        def _():
            send(work.at[3 - c], crecv.at[2 * c], 1, 2, sib)
            arrived(sc0r, 0)
            m, t = merged([pair(sc0[...]), pair(sc0r[...])], e0)
            sc1[...] = packed(m, t)
            for k in range(4):
                sc1n[k] = narrow(sc1[k * 64 : (k + 1) * 64, :])
            for r in (3, 1, 2):
                device, gp = quad[r]
                send(sc1n.at[gp], sc1r.at[r - 1], 2, 3, device)

        return carry

    lax.fori_loop(0, 3, pool, 0)

    def core_sum(k, b):
        both = e0[0] * work[b] + e0[1] * crecv[k]
        csum[k] = both.reshape(4, 8, 8, 128)

    arrived(crecv.at[pl.ds(outer, 2)], 1)
    for i in range(2):
        core_sum(outer + i, 4 * c + i)
    arrived(crecv.at[mid], 2)
    core_sum(mid, 2 + c)

    def quad_in(i):
        d = distance(i)
        for r in (3, 1, 2):
            device, gp = quad[r]
            send(csum.at[:, gp, (h + d) % 8], s1recv.at[r - 1, d], 3, QUAD_IN + d, device)

    each(8, quad_in)
    arrived(sc1r, 3)
    m, t = merged([pair(sc1[pl.ds(pl.multiple_of(g * 64, 64), 64), :])] + [wide(sc1r[i], 0, 64) for i in range(3)], e1)
    sc2[0] = narrow(packed(m, t))

    def scalars_in(i):
        d = distance(i)
        send(sc2.at[0], sc2r.at[d - 1], 4, 4, ring(d))

    each(7, scalars_in)

    def quad_sum(d):
        hp = (h + d) % 8
        rows = pl.ds(pl.multiple_of(hp * 8, 8), 8)
        arrived(s1recv.at[:, d], QUAD_IN + d)
        acc = e1[0, rows, :] * csum[:, g, hp]
        for i in range(3):
            acc = acc + e1[i + 1, rows, :] * s1recv[i, d]
        s1sum[d] = acc

    def ring_in(i):
        d = distance(i)
        quad_sum(d)
        send(s1sum.at[d], s2recv.at[d - 1], 5, 5, ring(d))

    each(7, ring_in)
    quad_sum(0)

    arrived(sc2r, 4)
    m, t = merged([wide(r, h * 8, 8) for r in [sc2[0]] + [sc2r[i] for i in range(7)]], e2)
    lse = m * LN2 + jnp.log(t)
    spot = h * 8 + lax.broadcasted_iota(jnp.int32, (8, 128), 0)
    hit = (lane[:8] == spot) | (lane[:8] == spot + 64)
    lse_own[0] = jnp.sum(jnp.where(hit, lse, 0.0), axis=0, keepdims=True)
    inv = 1.0 / t
    mine = pl.ds(3 * c, 3)
    arrived(s2recv, 5)
    acc = e2[0] * s1sum[0]
    for i in range(7):
        acc = acc + e2[i + 1] * s2recv[i]
    final[mine, g, h] = acc * inv
    piece = final.at[mine, g, h]
    each(7, lambda i: send(piece, piece, 7, RING_OUT + distance(i), ring(distance(i))))

    def quad_out(d):
        piece = final.at[mine, g, (h - d + 8) % 8]
        for r in (3, 1, 2):
            send(piece, piece, 8, QUAD_OUT + d, quad[r][0])

    def ring_out(i):
        d = distance(6 - i)
        arrived(s2recv.at[0], RING_OUT + d)
        quad_out(d)

    quad_out(0)

    def lse_out_ring(i):
        d = distance(i)
        send(lse_own.at[0], lser.at[d - 1], 6, 6, ring(d))

    each(7, lse_out_ring)
    each(7, ring_out)
    arrived(lser, 6)
    row = lse_own[0]
    for i in range(7):
        row = row + lser[i]
    lsen[g] = row
    for r in (3, 1, 2):
        send(lsen.at[g], lsen.at[g], 9, 7, quad[r][0])

    def sibling_out(i):
        d = distance(7 - i)
        arrived(s1recv.at[:, 0], QUAD_OUT + d)
        piece = final.at[mine, :, (h - d + 8) % 8]
        send(piece, piece, 10, 8, sib)

    each(8, sibling_out)

    arrived(sc1r, 7)
    for i in range(2):
        low = lane[:1] < 64
        lse_out[i : i + 1, :] = jnp.where(low, lsen[2 * i], lsen[2 * i + 1])
    arrived(crecv, 8)

    for i, block in enumerate(SPAN):
        part = nrecv.at[:, block]
        pltpu.make_async_copy(part, part, nsend.at[i]).wait()
    for stage, ref in enumerate((sc0r, crecv, sc1r, s1recv, sc2r, s2recv, sc2r, s2recv, s1recv, sc1r, crecv)):
        pltpu.make_async_copy(ref, ref, ssem.at[stage]).wait()


def write(norm, lse, parts, norm_out, lse_out, pooled_out, sem):
    copies = [
        pltpu.make_async_copy(parts.at[b], pooled_out.at[:, :, :, pl.ds(b * 128, 128)], sem.at[b])
        for b in range(6)
    ]
    copies.append(pltpu.make_async_copy(norm, norm_out, sem.at[6]))
    copies.append(pltpu.make_async_copy(lse, lse_out, sem.at[7]))
    for copy in copies:
        copy.start()
    for copy in copies:
        copy.wait()


def body(gallery, bank, test):
    vm = pltpu.VMEM
    dma = pltpu.SemaphoreType.DMA
    norm, lse, parts = pl.pallas_call(
        kernel,
        out_shape=(
            vm((CLIPS // 128, 128), F32),
            vm((TESTQ // 128, 128), F32),
            vm((6, 4, 8, 8, 128), F32),
        ),
        in_specs=[pl.BlockSpec(memory_space=pl.ANY)] * 3,
        out_specs=(pl.BlockSpec(memory_space=pltpu.VMEM),) * 3,
        scratch_shapes=[
            vm((CLIPS, D), BF16),
            vm((BANKQ, D), BF16),
            vm((TESTQ, D), BF16),
            vm((TESTQ, CLIPS), F32),
            vm((TESTQ, CLIPS), BF16),
            vm((CLIPS // 128, 128), F32),
            vm((7, CLIPS // 128, 128), F32),
            vm((CLIPS // 128, 128), F32),
            vm((6, TESTQ, 128), F32),
            vm((3, TESTQ, 128), F32),
            vm((3, 4, 8, 8, 128), F32),
            vm((3, 8, 3, 8, 128), F32),
            vm((8, 3, 8, 128), F32),
            vm((7, 3, 8, 128), F32),
            vm((TESTQ, 128), F32),
            vm((TESTQ, 128), F32),
            vm((TESTQ, 128), F32),
            vm((4, 1, 128), F32),
            vm((3, 1, 128), F32),
            vm((1, 1, 128), F32),
            vm((7, 1, 128), F32),
            vm((1, 1, 128), F32),
            vm((7, 1, 128), F32),
            vm((4, 1, 128), F32),
            vm((2, TESTQ, 128), F32),
            vm((4, 64, 128), F32),
            vm((8, 8, 128), F32),
            dma((PARTS + 2,)),
            dma((2,)),
            dma((33,)),
            dma((2,)),
            dma((11,)),
        ],
        compiler_params=pltpu.CompilerParams(
            collective_id=0, has_side_effects=True, vmem_limit_bytes=52 * 2**20
        ),
    )(*(pltpu.with_memory_space_constraint(a, pltpu.HBM) for a in (gallery, bank, test)))
    norm, lse, pooled = pl.pallas_call(
        write,
        out_shape=tuple(jax.ShapeDtypeStruct(s, F32) for s in (norm.shape, lse.shape, (4, 8, 8, D))),
        in_specs=[pl.BlockSpec(memory_space=pltpu.VMEM)] * 3,
        out_specs=(pl.BlockSpec(memory_space=pl.ANY),) * 3,
        scratch_shapes=[dma((8,))],
        compiler_params=pltpu.CompilerParams(vmem_limit_bytes=8 * 2**20),
    )(*(pltpu.with_memory_space_constraint(a, pltpu.VMEM) for a in (norm, lse, parts)))
    return norm.reshape(CLIPS), lse.reshape(TESTQ), pooled.reshape(TESTQ, D)


def solution(mesh):
    placed = (P("gal", None), P("qry", None), P("qry", None))
    return jax.shard_map(
        body,
        mesh=mesh,
        in_specs=placed,
        out_specs=(P("gal"), P("qry"), P("qry", None)),
        check_vma=False,
    )
```

```python
import functools
import math

import jax
import jax.numpy as jnp
from jax import lax
from jax.experimental import pallas as pl
from jax.experimental.pallas import tpu as pltpu
from jax.sharding import PartitionSpec as P

MESH = pl.DeviceIdType.MESH
F32 = jnp.float32
BF16 = jnp.bfloat16
LOG2E = math.log2(math.e)
LN2 = math.log(2.0)
NT = (((1,), (1,)), ((), ()))
CLIPS, BANKQ, TESTQ, D = 4096, 512, 256, 768
PARTS = 4
PC = CLIPS // PARTS
PR = PC // 128
SPAN = (pl.ds(0, CLIPS // 128 - PR), pl.ds(CLIPS // 128 - PR, PR))
QUAD_IN, RING_OUT, QUAD_OUT = 9, 17, 25


def kernel(
    gallery, bank, test, norm_out, lse_out, final,
    gal, bnk, tst, raw, wts, nloc, nrecv, n2, work, crecv, csum, s1recv, s1sum, s2recv,
    sc0, sc0r, sc1, sc1n, sc1r, sc2, sc2r, lse_own, lser, lsen, e0, e1, e2,
    lsem, nsem, rsem, nsend, ssem,
):
    me, q = lax.axis_index("gal"), lax.axis_index("qry")
    z, y, c = me // 4, (me // 2) % 2, me % 2
    zp, h = z % 2, z // 2
    g = y * 2 + zp

    def at(z_, y_, c_):
        return {"gal": z_ * 4 + y_ * 2 + c_}

    sib = at(z, y, 1 - c)
    zf, yf = z + 1 - 2 * zp, 1 - y
    quad = {
        1: (at(zf, y, c), y * 2 + 1 - zp),
        2: (at(z, yf, c), yf * 2 + zp),
        3: (at(zf, yf, c), yf * 2 + 1 - zp),
    }

    def ring(d):
        return at(((h + d) % 8) * 2 + zp, y, c)

    def panel(d):
        return {"qry": (q + d) % 8}

    def distance(i):
        return 4 + (i + 1) // 2 * (1 - 2 * (i % 2))

    def each(n, step):
        def run(i, carry):
            step(i)
            return carry

        lax.fori_loop(0, n, run, 0)

    loads = [pltpu.make_async_copy(bank, bnk, lsem.at[PARTS])]
    for j in range(PARTS):
        rows = pl.ds(j * PC, PC)
        loads.append(pltpu.make_async_copy(gallery.at[rows], gal.at[rows], lsem.at[j]))
    loads.append(pltpu.make_async_copy(test, tst, lsem.at[PARTS + 1]))
    for load in loads:
        load.start()

    barrier = pltpu.get_barrier_semaphore()

    def greet(device):
        pl.semaphore_signal(barrier, inc=1, device_id=device, device_id_type=MESH)

    def greet_far(i):
        greet(ring(distance(i)))
        greet(panel(distance(i)))

    each(7, greet_far)
    for device in [sib] + [p for p, _ in quad.values()]:
        greet(device)

    def send(src, dst, stage, slot, device):
        pltpu.make_async_remote_copy(
            src_ref=src, dst_ref=dst, send_sem=ssem.at[stage], recv_sem=rsem.at[slot],
            device_id=device, device_id_type=MESH,
        ).start()

    def arrived(ref, slot):
        pltpu.make_async_copy(ref, ref, rsem.at[slot]).wait()

    c2 = 5.0 / math.sqrt(D) * LOG2E
    loads[0].wait()

    def send_part(i):
        def step(k):
            d = distance(k)
            pltpu.make_async_remote_copy(
                src_ref=nloc.at[SPAN[i]], dst_ref=nrecv.at[d - 1, SPAN[i]],
                send_sem=nsend.at[i], recv_sem=nsem.at[i],
                device_id=panel(d), device_id_type=MESH,
            ).start()

        each(7, step)

    def bank_part(j, carry):
        rows = pl.ds(pl.multiple_of(j * PC, PC), PC)
        pltpu.make_async_copy(gallery.at[rows], gal.at[rows], lsem.at[j]).wait()
        r = lax.dot_general(bnk[...], gal[rows, :], NT, preferred_element_type=F32)
        m = jnp.max(r, axis=0, keepdims=True)
        s = jnp.sum(jnp.exp2((r - m) * c2), axis=0, keepdims=True)
        l2 = m * c2 + jnp.log(s) * LOG2E
        for i in range(PR):
            nloc[pl.ds(j * PR + i, 1), :] = l2[:, i * 128 : (i + 1) * 128]

        @pl.when(j == PARTS - 2)
        def _():
            pl.semaphore_wait(barrier, 18)
            send_part(0)

        return carry

    lax.fori_loop(0, PARTS, bank_part, 0)
    send_part(1)

    loads[-1].wait()

    def test_part(j, carry):
        rows = pl.ds(pl.multiple_of(j * 2048, 2048), 2048)
        raw[:, rows] = lax.dot_general(tst[...], gal[rows, :], NT, preferred_element_type=F32)
        return carry

    lax.fori_loop(0, CLIPS // 2048, test_part, 0)

    peak = jnp.full((TESTQ, 128), -jnp.inf, F32)
    for i, block in enumerate(SPAN):
        part = nrecv.at[:, block]
        pltpu.make_async_copy(part, part, nsem.at[i]).wait()
        own = nloc[block, :]
        m = own
        for d in range(7):
            m = jnp.maximum(m, nrecv[d, block, :])
        s = jnp.exp2(own - m)
        for d in range(7):
            s = s + jnp.exp2(nrecv[d, block, :] - m)
        n2[block, :] = m + jnp.log(s) * LOG2E

        def shift(i, peak):
            lanes = pl.ds(pl.multiple_of(i * 128, 128), 128)
            x = raw[:, lanes] * c2 - n2[pl.ds(i, 1), :]
            raw[:, lanes] = x
            return jnp.maximum(peak, x)

        peak = lax.fori_loop(block.start, block.start + block.size, shift, peak, unroll=2)
    peak = jnp.max(peak, axis=1, keepdims=True)
    norm_out[...] = n2[...] * LN2

    there = 4 * (1 - c)
    ahead = pl.ds(pl.multiple_of(there * 128, 512), 256)
    work[there] = jnp.zeros((TESTQ, 128), F32)
    work[there + 1] = jnp.zeros((TESTQ, 128), F32)

    def weigh(i, total):
        for k in range(8):
            lanes = pl.ds(pl.multiple_of(i * 1024 + k * 128, 128), 128)
            e = jnp.exp2(raw[:, lanes] - peak)
            wts[:, lanes] = e.astype(BF16)
            total = total + e
        rows = pl.ds(pl.multiple_of(i * 1024, 1024), 1024)
        out = jnp.dot(wts[:, rows], gal[rows, ahead], preferred_element_type=F32)
        work[there] += out[:, :128]
        work[there + 1] += out[:, 128:]
        return total

    total = lax.fori_loop(0, CLIPS // 1024, weigh, jnp.zeros((TESTQ, 128), F32))
    total = jnp.sum(total, axis=1, keepdims=True)

    def packed(m, t):
        lane = lax.broadcasted_iota(jnp.int32, m.shape, 1)
        return jnp.where(lane < 64, m, t)

    def spread(a, lane):
        return jnp.broadcast_to(a[:, lane : lane + 1], a.shape)

    def merged(pairs, scales):
        m = functools.reduce(jnp.maximum, [mi for mi, _ in pairs])
        t = None
        for i, (mi, ti) in enumerate(pairs):
            e = jnp.exp2(mi - m)
            scales[i] = e
            t = e * ti if t is None else t + e * ti
        return m, t

    def pair(tile):
        return spread(tile, 0), spread(tile, 64)

    sub = lax.broadcasted_iota(jnp.int32, (64, 128), 0)
    lane = lax.broadcasted_iota(jnp.int32, (64, 128), 1)

    def narrow(tile):
        hit = (lane == sub) | (lane == sub + 64)
        return jnp.sum(jnp.where(hit, tile, 0.0), axis=0, keepdims=True)

    def wide(row, first, count):
        spot = first + lax.broadcasted_iota(jnp.int32, (count, 128), 0)

        def column(shift):
            x = jnp.where(lane[:count] == spot + shift, jnp.broadcast_to(row, (count, 128)), 0.0)
            return jnp.broadcast_to(jnp.sum(x, axis=1, keepdims=True), (count, 128))

        return column(0), column(64)

    sc0[...] = packed(jnp.broadcast_to(peak, (TESTQ, 128)), jnp.broadcast_to(total, (TESTQ, 128)))
    send(sc0, sc0r, 0, 0, sib)
    send(work.at[pl.ds(there, 2)], crecv.at[pl.ds(1 - c, 2)], 1, 1, sib)

    mid, outer = 2 - 2 * c, c

    def pool(i, carry):
        tile = 2 - 2 * c + i * (2 * c - 1)
        lanes = pl.ds(pl.multiple_of(tile * 256, 256), 256)
        out = jnp.dot(wts[...], gal[:, lanes], preferred_element_type=F32)
        work[2 * tile] = out[:, :128]
        work[2 * tile + 1] = out[:, 128:]

        @pl.when(i == 1)
        def _():
            send(work.at[3 - c], crecv.at[2 * c], 1, 2, sib)
            arrived(sc0r, 0)
            m, t = merged([pair(sc0[...]), pair(sc0r[...])], e0)
            sc1[...] = packed(m, t)
            for k in range(4):
                sc1n[k] = narrow(sc1[k * 64 : (k + 1) * 64, :])
            for r in (3, 1, 2):
                device, gp = quad[r]
                send(sc1n.at[gp], sc1r.at[r - 1], 2, 3, device)

        return carry

    lax.fori_loop(1, 3, pool, 0)

    def core_sum(k, b):
        both = e0[0] * work[b] + e0[1] * crecv[k]
        csum[k] = both.reshape(4, 8, 8, 128)

    arrived(crecv.at[pl.ds(outer, 2)], 1)
    for i in range(2):
        core_sum(outer + i, 4 * c + i)
    arrived(crecv.at[mid], 2)
    core_sum(mid, 2 + c)

    def quad_in(i):
        d = distance(i)
        for r in (3, 1, 2):
            device, gp = quad[r]
            send(csum.at[:, gp, (h + d) % 8], s1recv.at[r - 1, d], 3, QUAD_IN + d, device)

    each(8, quad_in)
    arrived(sc1r, 3)
    m, t = merged([pair(sc1[pl.ds(pl.multiple_of(g * 64, 64), 64), :])] + [wide(sc1r[i], 0, 64) for i in range(3)], e1)
    sc2[0] = narrow(packed(m, t))

    def scalars_in(i):
        d = distance(i)
        send(sc2.at[0], sc2r.at[d - 1], 4, 4, ring(d))

    each(7, scalars_in)

    def quad_sum(d):
        hp = (h + d) % 8
        rows = pl.ds(pl.multiple_of(hp * 8, 8), 8)
        arrived(s1recv.at[:, d], QUAD_IN + d)
        acc = e1[0, rows, :] * csum[:, g, hp]
        for i in range(3):
            acc = acc + e1[i + 1, rows, :] * s1recv[i, d]
        s1sum[d] = acc

    def ring_in(i):
        d = distance(i)
        quad_sum(d)
        send(s1sum.at[d], s2recv.at[d - 1], 5, 5, ring(d))

    each(7, ring_in)
    quad_sum(0)

    arrived(sc2r, 4)
    m, t = merged([wide(r, h * 8, 8) for r in [sc2[0]] + [sc2r[i] for i in range(7)]], e2)
    lse = m * LN2 + jnp.log(t)
    spot = h * 8 + lax.broadcasted_iota(jnp.int32, (8, 128), 0)
    hit = (lane[:8] == spot) | (lane[:8] == spot + 64)
    lse_own[0] = jnp.sum(jnp.where(hit, lse, 0.0), axis=0, keepdims=True)
    inv = 1.0 / t
    mine = pl.ds(3 * c, 3)
    arrived(s2recv, 5)
    acc = e2[0] * s1sum[0]
    for i in range(7):
        acc = acc + e2[i + 1] * s2recv[i]
    final[mine, g, h] = acc * inv
    piece = final.at[mine, g, h]
    each(7, lambda i: send(piece, piece, 7, RING_OUT + distance(i), ring(distance(i))))

    def quad_out(d):
        piece = final.at[mine, g, (h - d + 8) % 8]
        for r in (3, 1, 2):
            send(piece, piece, 8, QUAD_OUT + d, quad[r][0])

    def ring_out(i):
        d = distance(6 - i)
        arrived(s2recv.at[0], RING_OUT + d)
        quad_out(d)

    quad_out(0)

    def lse_out_ring(i):
        d = distance(i)
        send(lse_own.at[0], lser.at[d - 1], 6, 6, ring(d))

    each(7, lse_out_ring)
    each(7, ring_out)
    arrived(lser, 6)
    row = lse_own[0]
    for i in range(7):
        row = row + lser[i]
    lsen[g] = row
    for r in (3, 1, 2):
        send(lsen.at[g], lsen.at[g], 9, 7, quad[r][0])

    def sibling_out(i):
        d = distance(7 - i)
        arrived(s1recv.at[:, 0], QUAD_OUT + d)
        piece = final.at[mine, :, (h - d + 8) % 8]
        send(piece, piece, 10, 8, sib)

    each(8, sibling_out)

    arrived(sc1r, 7)
    for i in range(2):
        low = lane[:1] < 64
        lse_out[i : i + 1, :] = jnp.where(low, lsen[2 * i], lsen[2 * i + 1])
    arrived(crecv, 8)

    for i, block in enumerate(SPAN):
        part = nrecv.at[:, block]
        pltpu.make_async_copy(part, part, nsend.at[i]).wait()
    for stage, ref in enumerate((sc0r, crecv, sc1r, s1recv, sc2r, s2recv, sc2r, s2recv, s1recv, sc1r, crecv)):
        pltpu.make_async_copy(ref, ref, ssem.at[stage]).wait()


def write(norm, lse, parts, norm_out, lse_out, pooled_out, sem):
    copies = [
        pltpu.make_async_copy(parts.at[b], pooled_out.at[:, :, :, pl.ds(b * 128, 128)], sem.at[b])
        for b in range(6)
    ]
    copies.append(pltpu.make_async_copy(norm, norm_out, sem.at[6]))
    copies.append(pltpu.make_async_copy(lse, lse_out, sem.at[7]))
    for copy in copies:
        copy.start()
    for copy in copies:
        copy.wait()


def body(gallery, bank, test):
    vm = pltpu.VMEM
    dma = pltpu.SemaphoreType.DMA
    norm, lse, parts = pl.pallas_call(
        kernel,
        out_shape=(
            vm((CLIPS // 128, 128), F32),
            vm((TESTQ // 128, 128), F32),
            vm((6, 4, 8, 8, 128), F32),
        ),
        in_specs=[pl.BlockSpec(memory_space=pl.ANY)] * 3,
        out_specs=(pl.BlockSpec(memory_space=pltpu.VMEM),) * 3,
        scratch_shapes=[
            vm((CLIPS, D), BF16),
            vm((BANKQ, D), BF16),
            vm((TESTQ, D), BF16),
            vm((TESTQ, CLIPS), F32),
            vm((TESTQ, CLIPS), BF16),
            vm((CLIPS // 128, 128), F32),
            vm((7, CLIPS // 128, 128), F32),
            vm((CLIPS // 128, 128), F32),
            vm((6, TESTQ, 128), F32),
            vm((3, TESTQ, 128), F32),
            vm((3, 4, 8, 8, 128), F32),
            vm((3, 8, 3, 8, 128), F32),
            vm((8, 3, 8, 128), F32),
            vm((7, 3, 8, 128), F32),
            vm((TESTQ, 128), F32),
            vm((TESTQ, 128), F32),
            vm((TESTQ, 128), F32),
            vm((4, 1, 128), F32),
            vm((3, 1, 128), F32),
            vm((1, 1, 128), F32),
            vm((7, 1, 128), F32),
            vm((1, 1, 128), F32),
            vm((7, 1, 128), F32),
            vm((4, 1, 128), F32),
            vm((2, TESTQ, 128), F32),
            vm((4, 64, 128), F32),
            vm((8, 8, 128), F32),
            dma((PARTS + 2,)),
            dma((2,)),
            dma((33,)),
            dma((2,)),
            dma((11,)),
        ],
        compiler_params=pltpu.CompilerParams(
            collective_id=0, has_side_effects=True, vmem_limit_bytes=52 * 2**20
        ),
    )(*(pltpu.with_memory_space_constraint(a, pltpu.HBM) for a in (gallery, bank, test)))
    norm, lse, pooled = pl.pallas_call(
        write,
        out_shape=tuple(jax.ShapeDtypeStruct(s, F32) for s in (norm.shape, lse.shape, (4, 8, 8, D))),
        in_specs=[pl.BlockSpec(memory_space=pltpu.VMEM)] * 3,
        out_specs=(pl.BlockSpec(memory_space=pl.ANY),) * 3,
        scratch_shapes=[dma((8,))],
        compiler_params=pltpu.CompilerParams(vmem_limit_bytes=8 * 2**20),
    )(*(pltpu.with_memory_space_constraint(a, pltpu.VMEM) for a in (norm, lse, parts)))
    return norm.reshape(CLIPS), lse.reshape(TESTQ), pooled.reshape(TESTQ, D)


def solution(mesh):
    placed = (P("gal", None), P("qry", None), P("qry", None))
    return jax.shard_map(
        body,
        mesh=mesh,
        in_specs=placed,
        out_specs=(P("gal"), P("qry"), P("qry", None)),
        check_vma=False,
    )
```
